32 devices in a mesh: pipe: 4 (over y, x), ctx: 4 (over z), head: 2 (over core).
Axes of the slice: x: 2, y: 2, z: 4, core: 2. Of those that a mesh axis runs over, the one named last changes fastest.
Arguments:
- queries: bfloat16 [4, 512, 64, 128], P('pipe', 'ctx', 'head'), may hold values from -160 to 160
- key_heads: bfloat16 [4, 512, 8, 128], P('pipe', 'ctx', 'head'), may hold values from -6 to 6
- value_heads: bfloat16 [4, 512, 8, 128], P('pipe', 'ctx', 'head'), may hold values from -6 to 6
- forward_out: bfloat16 [4, 512, 64, 128], P('pipe', 'ctx', 'head'), may hold values from -4 to 4
- output_grad: bfloat16 [4, 512, 64, 128], P('pipe', 'ctx', 'head'), may hold values from -6 to 6
- block_order: int32 [8], replicated, may hold values from 0 to 7, each once
Outputs:
- key_grad: bfloat16 [4, 512, 8, 128], P('pipe', 'ctx', 'head')
- value_grad: bfloat16 [4, 512, 8, 128], P('pipe', 'ctx', 'head')
- handed: bfloat16 [4, 512, 64, 128], P('pipe', 'ctx', 'head')
The draws below stay inside these ranges and needn't reach their ends.
Inputs may be any that keep to these rules, and one draw needn't show every extreme that they name: `block_order`: every half-block number appears exactly once.
All inputs are finite; a program needn't handle non-finite values.
Results may differ from the reference program's by a relative error of at most 0.012.
The reference program's roundings to bfloat16 on the way count: a program that leaves them out, or rounds other values in their place, can miss the bound.
Values may be sent and summed in bfloat16 or wider, within the bound.
No kernel may reach another device: no remote copies, remote signals or barrier semaphores. Data moves between devices by JAX's collectives and lax.ppermute only.
A program may use at most 64 MiB of HBM per device.

```python
import math
import jax
import jax.numpy as jnp
from jax import lax

QH = 64
KVH = 8
HD = 128
HALF = 64
SEQ = 512
N_PIPE = 4
N_CTX = 4


def draw_common(key):
    base = jax.random.fold_in(key, 11)
    key_draw, query_draw = jax.random.split(base, 2)
    key_vals = jnp.clip(jax.random.normal(key_draw, (N_PIPE, SEQ, KVH, HD), jnp.float32), -6.0, 6.0)
    query_vals = jnp.clip(jax.random.normal(query_draw, (N_PIPE, SEQ, QH, HD), jnp.float32), -6.0, 6.0)
    return (key_vals, query_vals)


def draw_queries(key, part):
    key_vals, query_vals = draw_common(key)
    return query_vals.astype(jnp.bfloat16)


def draw_key_heads(key, part):
    key_vals, query_vals = draw_common(key)
    return key_vals.astype(jnp.bfloat16)


def block_scale(key, extent, cuts, low, top_value):
    def one(axis_at, shards_of):
        steps = jax.random.uniform(jax.random.fold_in(jax.random.fold_in(key, 6), axis_at), (shards_of,), jnp.float32, low / len(cuts), top_value / len(cuts))
        return jnp.repeat(jnp.exp(steps), extent[axis_at] // shards_of).reshape((-1,) + (1,) * (len(extent) - axis_at - 1))

    level = one(*cuts[0])
    for cut in cuts[1:]:
        level = level * one(*cut)
    return level


def gaussian(key, extent, scale, limit, shards=(), kind=jnp.bfloat16):
    values = scale * jax.random.normal(key, extent, jnp.float32)
    if shards:
        values = values * block_scale(key, extent, shards, -0.22, 0.18)
    return jnp.clip(values, -limit, limit).astype(kind)


def setup_inputs(seed: int = 0) -> dict:
    keys = jax.random.split(jax.random.key(seed), 7)
    queries = draw_queries(jax.random.fold_in(keys[6], 71), 0)
    key_heads = draw_key_heads(jax.random.fold_in(keys[6], 71), 0)
    value_heads = gaussian(keys[2], (N_PIPE, SEQ, KVH, HD), 1.0, 6.0, ((0, 4), (1, 4), (2, 2)))
    forward_out = gaussian(keys[3], (N_PIPE, SEQ, QH, HD), 0.5, 4.0, ((0, 4), (1, 4), (2, 2)))
    output_grad = gaussian(keys[4], (N_PIPE, SEQ, QH, HD), 1.0, 6.0, ((0, 4), (1, 4), (2, 2)))
    block_order = jax.random.permutation(keys[5], 2 * N_CTX).astype(jnp.int32)
    return {"queries": queries, "key_heads": key_heads, "value_heads": value_heads, "forward_out": forward_out, "output_grad": output_grad, "block_order": block_order}


NEG = -1e+30

def hadamard(size_in):
    indices = jnp.arange(size_in, dtype=jnp.int32)
    parity = jnp.zeros((size_in, size_in), jnp.int32)
    for bit_place in range(size_in.bit_length() - 1):
        digit = indices // 2 ** bit_place % 2
        parity = parity + digit[:, None] * digit[None, :]
    parity = parity % 2
    return (1.0 - 2.0 * parity.astype(jnp.float32)) / math.sqrt(size_in)

def rotate(values, rotation):
    return jnp.dot(values.astype(jnp.float32), rotation, precision=lax.Precision.HIGHEST).astype(jnp.bfloat16)

def reference(queries, key_heads, value_heads, forward_out, output_grad, block_order):
    rotation = hadamard(HD)
    score_scale = 1.0 / math.sqrt(HD)
    per_group = QH // KVH
    seq_rows = jnp.arange(SEQ, dtype=jnp.int32)
    positions = jnp.repeat(block_order.astype(jnp.int32), HALF) * HALF + seq_rows % HALF
    visible = positions[None, :] <= positions[:, None]

    def stack_query(array):
        return array.reshape(N_PIPE, SEQ, KVH, per_group, HD).transpose(0, 2, 1, 3, 4).reshape(N_PIPE * KVH, SEQ, per_group, HD)

    def stack_key(array):
        return array.transpose(0, 2, 1, 3).reshape(N_PIPE * KVH, SEQ, HD)

    def one_group(items):
        q_in, k_in, v_in, o_in, g_in = items
        q_rot = rotate(q_in, rotation)
        k_rot = rotate(k_in, rotation)
        scores = jnp.einsum('igd,jd->gij', q_rot.astype(jnp.float32), k_rot.astype(jnp.float32)) * score_scale
        scores = jnp.where(visible[None], scores, NEG)
        row_top = lax.optimization_barrier(jnp.max(scores, -1, keepdims=True))
        row_lse = row_top + jnp.log(lax.optimization_barrier(jnp.sum(jnp.exp(scores - row_top), -1, keepdims=True)))
        weights = jnp.exp(scores - row_lse)
        grad_f = g_in.astype(jnp.float32)
        row_delta = lax.optimization_barrier(jnp.sum(grad_f * o_in.astype(jnp.float32), -1)).T
        weight_grad = jnp.einsum('igd,jd->gij', grad_f, v_in.astype(jnp.float32))
        dscore = (weights * (weight_grad - row_delta[..., None])).astype(jnp.bfloat16)
        weights_low = weights.astype(jnp.bfloat16)
        dq_rot = jnp.einsum('gij,jd->igd', dscore.astype(jnp.float32), k_rot.astype(jnp.float32)) * score_scale
        dk_rot = jnp.einsum('gij,igd->jd', dscore.astype(jnp.float32), q_rot.astype(jnp.float32)) * score_scale
        dv_sum = jnp.einsum('gij,igd->jd', weights_low.astype(jnp.float32), grad_f)
        dq_full = jnp.dot(dq_rot.reshape(-1, HD), rotation.T, precision=lax.Precision.HIGHEST).reshape(SEQ, per_group, HD)
        dk_full = jnp.dot(dk_rot, rotation.T, precision=lax.Precision.HIGHEST)
        handed_here = (grad_f + dq_full).astype(jnp.bfloat16)
        return (dk_full.astype(jnp.bfloat16), dv_sum.astype(jnp.bfloat16), handed_here)
    dk_all, dv_all, handed_all = lax.map(one_group, (stack_query(queries), stack_key(key_heads), stack_key(value_heads), stack_query(forward_out), stack_query(output_grad)))
    key_grad = dk_all.reshape(N_PIPE, KVH, SEQ, HD).transpose(0, 2, 1, 3)
    value_grad = dv_all.reshape(N_PIPE, KVH, SEQ, HD).transpose(0, 2, 1, 3)
    handed_all = handed_all.reshape(N_PIPE, KVH, SEQ, per_group, HD).transpose(0, 2, 1, 3, 4).reshape(N_PIPE, SEQ, QH, HD)
    handed = jnp.concatenate([handed_all[1:], jnp.zeros_like(handed_all[:1])], axis=0)
    return (key_grad, value_grad, handed)
```

```python
import functools
import math

import jax
import jax.numpy as jnp
from jax import lax
from jax.experimental import pallas as pl
from jax.experimental.pallas import tpu as pltpu
from jax.sharding import PartitionSpec as P

NEG = -1e30
STAGES = 2
WORK = 2**20
DQ_WORK = 2**32
F32 = jnp.float32
BF16 = jnp.bfloat16


def signs(size):
    row = lax.broadcasted_iota(jnp.int32, (size, size), 0)
    col = lax.broadcasted_iota(jnp.int32, (size, size), 1)
    bits = row & col
    for step in (4, 2, 1):
        bits = bits ^ (bits >> step)
    return (1 - 2 * (bits & 1)).astype(F32).astype(BF16)


def dot(a, b, contract):
    return lax.dot_general(a, b, (contract, ((), ())), preferred_element_type=F32)


def nn(a, b):
    return dot(a, b, ((1,), (0,)))


def nt(a, b):
    return dot(a, b, ((1,), (1,)))


def split(x):
    high = x.astype(BF16)
    return high, (x - high.astype(F32)).astype(BF16)


def prep_kernel(groups, per_stage, k_hbm, v_hbm, *rest):
    outs, (rows_ref, k_ref, v_ref, sems) = rest[:-4], rest[-4:]
    copies = [
        pltpu.make_async_copy(source, target, sems.at[at])
        for at, (source, target) in enumerate(((k_hbm, k_ref), (v_hbm, v_ref)))
    ]
    for copy in copies:
        copy.start()
    tokens = k_ref.shape[0] // groups
    size = k_ref.shape[1]
    sign = signs(size)
    for part, copy in enumerate(copies):
        copy.wait()
        if part == 0:
            rows = nn(k_ref[...], sign) * (1.0 / math.sqrt(size))
        else:
            rows = v_ref[...].astype(F32)
        rows_ref[...] = rows
        for group in range(groups):
            picked = rows_ref[pl.ds(group, tokens, stride=groups), :].astype(BF16)
            outs[group // per_stage][part, group % per_stage] = picked


def finish_kernel(groups, per_stage, terms, *refs):
    count = groups // per_stage * terms
    parts, outs, rows_ref = refs[:count], refs[count:-1], refs[-1]
    tokens = parts[0].shape[2]
    for part in range(2):
        for group in range(groups):
            first = group // per_stage * terms
            rows = [ref[part, group % per_stage].astype(F32) for ref in parts[first : first + terms]]
            rows_ref[pl.ds(group, tokens, stride=groups), :] = sum(rows[1:], rows[0])
        outs[part][...] = rows_ref[...].astype(BF16)


def ring_order(count):
    return [0] + [at for at in range(count) if at % 2] + [at for at in range(count - 1, 0, -1) if at % 2 == 0]


def ring_place(count, place):
    odd = place & 1
    half = place >> 1
    return lax.rem(odd * (half + 1) + (1 - odd) * (count - half), count)


def ring_device(count, ring):
    return jnp.where(ring <= count // 2, jnp.maximum(2 * ring - 1, 0), 2 * (count - ring))


def passed(value, axis, step):
    count = lax.axis_size(axis)
    order = ring_order(count)
    return lax.ppermute(
        value, axis, [(order[at], order[(at + step) % count]) for at in range(count)]
    )


def later_pass(block, up, down, axis):
    count = lax.axis_size(axis)
    blocks = {0: block, 1: up, count - 1: down}
    for step in range(2, count // 2 + 1):
        up = blocks[step] = passed(up, axis, 1)
        if 2 * step < count:
            down = blocks[count - step] = passed(down, axis, -1)
    return [blocks[step] for step in range(count)]


def added(a, b):
    return (a.astype(F32) + b.astype(F32)).astype(BF16)


def scatter_sums(parts, axis):
    count = lax.axis_size(axis)
    terms = [parts[0]]
    for step, longest in ((1, count // 2), (-1, (count - 1) // 2)):
        moving = None
        for distance in range(longest, 0, -1):
            part = parts[(-step * distance) % count]
            moving = passed(part if moving is None else added(moving, part), axis, step)
        terms.append(moving)
    return terms


def sides_kernel(stage, groups, q_hbm, g_hbm, o_hbm, q_side_ref, g_side_ref, in_ref, sems):
    _, _, half_rows, heads, size = in_ref.shape
    per_group = heads // groups
    copies = []
    for half in range(2):
        for part, source in enumerate((q_hbm, g_hbm, o_hbm)):
            piece = source.at[pl.ds(half * half_rows, half_rows), pl.ds(stage * heads, heads)]
            copies.append(
                pltpu.make_async_copy(piece, in_ref.at[half, part], sems.at[half * 3 + part])
            )
            copies[-1].start()
    rows = half_rows * per_group
    sign = signs(size)
    root = 1.0 / math.sqrt(size)
    row_offset = lax.broadcasted_iota(jnp.int32, (rows, size), 0) // per_group
    lane = lax.broadcasted_iota(jnp.int32, (rows, size), 1)
    hide = jnp.where(row_offset == lane, NEG, 0.0).astype(BF16)
    for half in range(2):
        for copy in copies[3 * half : 3 * half + 3]:
            copy.wait()
        q_all = nn(in_ref[half, 0].reshape(half_rows * heads, size), sign) * root
        q_all = q_all.reshape(half_rows, groups, per_group, size)
        g_all = in_ref[half, 1].astype(F32).reshape(half_rows, groups, per_group, size)
        o_all = in_ref[half, 2].astype(F32).reshape(half_rows, groups, per_group, size)
        for group in range(groups):
            grad = g_all[:, group].reshape(rows, size)
            product = grad * o_all[:, group].reshape(rows, size)
            product = -(product + pltpu.roll(product, size // 2, 1))
            high = product.astype(BF16).astype(F32)
            delta = jnp.where(lane < size // 2, high, product - high)
            q_side_ref[half, group, :, :size] = q_all[:, group].reshape(rows, size).astype(BF16)
            q_side_ref[half, group, :, size:] = hide
            g_side_ref[half, group, :, :size] = grad.astype(BF16)
            g_side_ref[half, group, :, size:] = delta.astype(BF16)


def chunked(keys, chunk, body, init):
    if keys == chunk:
        return body(0, init)
    return lax.fori_loop(0, keys // chunk, body, init)


def dq_kernel(blocks, order_ref, q_side_ref, g_side_ref, *refs):
    kv_refs, (handed_ref, probs_ref, dscore_ref) = refs[:blocks], refs[blocks : blocks + 3]
    score_ref, key_ref, val_ref, back_ref = refs[blocks + 3 :]
    _, groups, tokens, size = kv_refs[0].shape
    place = lax.axis_index("ctx")
    ring = ring_place(blocks, place)
    rows = q_side_ref.shape[2]
    half_rows = tokens // 2
    per_group = rows // half_rows
    keys = blocks * tokens
    chunk = 512
    root = 1.0 / math.sqrt(size)
    power = root * math.log2(math.e)
    sign = signs(size)

    def span(index):
        return pl.ds(pl.multiple_of(index * chunk, chunk), chunk)

    at_row = lax.broadcasted_iota(jnp.int32, (half_rows, size), 0)
    at_col = lax.broadcasted_iota(jnp.int32, (half_rows, size), 1)
    for block in range(blocks):
        source = ring_device(blocks, lax.rem(ring - block + blocks, blocks))
        at = pl.ds(block * tokens, tokens)
        for half in range(2):
            q_start = order_ref[place * 2 + half]
            for k_half in range(2):
                ahead = (order_ref[source * 2 + k_half] - q_start) * half_rows
                hidden = (at_row + ahead > at_col) & (at_col < half_rows)
                hidden = jnp.where(hidden, 1.0, 0.0).astype(BF16)
                k_at = pl.ds(block * tokens + k_half * half_rows, half_rows)
                for group in range(groups):
                    key_ref[half, group, k_at, size:] = hidden
        for group in range(groups):
            key = kv_refs[block][0, group]
            for half in range(2):
                key_ref[half, group, at, :size] = key
            val_ref[group, at, :size] = kv_refs[block][1, group]
            val_ref[group, at, size:] = jnp.ones((tokens, size), BF16)
            high, low = split(nt(sign, key) * (root * root))
            back_ref[group, :size, at] = high
            back_ref[group, size:, at] = low

    for half in range(2):
        results = []
        for group in range(groups):
            slot = group % 2
            q_side = q_side_ref.at[half, group]
            g_side = g_side_ref.at[half, group]
            row_at = pl.ds(half * rows, rows)

            def scores(index, top, half=half, group=group, slot=slot, q_side=q_side):
                part = nt(key_ref[half, group, span(index), :], q_side[...])
                score_ref[slot, span(index), :] = part
                return jnp.maximum(top, jnp.max(part.reshape(chunk // 8, 8, rows), axis=0))

            top = chunked(keys, chunk, scores, jnp.full((8, rows), NEG, F32))
            top = jnp.max(top, axis=0, keepdims=True)

            def weigh(index, total, slot=slot, top=top):
                part = jnp.exp2((score_ref[slot, span(index), :] - top) * power)
                score_ref[slot, span(index), :] = part
                return total + jnp.sum(part.reshape(chunk // 8, 8, rows), axis=0)

            total = chunked(keys, chunk, weigh, jnp.zeros((8, rows), F32))
            scale = 1.0 / jnp.sum(total, axis=0, keepdims=True)

            def grads(index, dq, group=group, slot=slot, scale=scale, g_side=g_side, row_at=row_at):
                probs = score_ref[slot, span(index), :] * scale
                change = nt(val_ref[group, span(index), :], g_side[...])
                dscore = (probs * change).astype(BF16)
                probs_ref[group, span(index), row_at] = probs.astype(BF16)
                dscore_ref[group, span(index), row_at] = dscore
                return dq + nn(back_ref[group, :, span(index)], dscore)

            dq = chunked(keys, chunk, grads, jnp.zeros((2 * size, rows), F32))
            dq = (dq[:size] + dq[size:]).T + g_side[:, :size].astype(F32)
            results.append(dq.reshape(half_rows, per_group, size))
        at = pl.ds(half * half_rows, half_rows)
        handed_ref[at] = jnp.concatenate(results, axis=1).astype(BF16)


def dkv_kernel(q_side_ref, g_side_ref, probs_ref, dscore_ref, *sum_refs):
    blocks = len(sum_refs)
    _, groups, tokens, size = sum_refs[0].shape
    rows = q_side_ref.shape[2]
    scale = 1.0 / size
    sign = signs(size)
    chunk = 512
    for first in range(0, blocks * tokens, chunk):
        for group in range(groups):
            at = pl.ds(first, chunk)
            dk = dv = None
            for half in range(2):
                row_at = pl.ds(half * rows, rows)
                dk_part = nn(dscore_ref[group, at, row_at], q_side_ref[half, group, :, :size])
                dv_part = nn(probs_ref[group, at, row_at], g_side_ref[half, group, :, :size])
                dk = dk_part if dk is None else dk + dk_part
                dv = dv_part if dv is None else dv + dv_part
            high, low = split(dk)
            dk = ((nn(high, sign) + nn(low, sign)) * scale).astype(BF16)
            dv = dv.astype(BF16)
            for row in range(0, chunk, tokens):
                out = sum_refs[(first + row) // tokens]
                out[0, group] = dk[row : row + tokens]
                out[1, group] = dv[row : row + tokens]


VMEM = pl.BlockSpec(memory_space=pltpu.VMEM)
HBM = pl.BlockSpec(memory_space=pltpu.HBM)
DMA = pltpu.SemaphoreType.DMA
SMEM = pl.BlockSpec(memory_space=pltpu.SMEM)


def call(kernel, name, outs, scratch, limit, work, args, smem=False):
    shapes = [jax.ShapeDtypeStruct(*out) for out in outs]
    return pl.pallas_call(
        kernel,
        in_specs=([SMEM] if smem else []) + [VMEM] * (len(args) - smem),
        out_specs=[VMEM] * len(outs),
        out_shape=shapes,
        scratch_shapes=scratch,
        compiler_params=pltpu.CompilerParams(vmem_limit_bytes=limit * 2**20),
        cost_estimate=pl.CostEstimate(flops=work, bytes_accessed=2**16, transcendentals=0),
        name=name,
    )(*args)


def in_hbm(value):
    return pltpu.with_memory_space_constraint(value, pltpu.HBM)


def make_sides(stage, stages, groups, queries, grads, saved):
    tokens, heads, size = queries.shape
    half_rows, heads = tokens // 2, heads // stages
    rows = half_rows * heads // groups
    shape = jax.ShapeDtypeStruct((2, groups, rows, 2 * size), BF16)
    return pl.pallas_call(
        functools.partial(sides_kernel, stage, groups),
        in_specs=[HBM] * 3,
        out_specs=[VMEM] * 2,
        out_shape=[shape] * 2,
        scratch_shapes=[pltpu.VMEM((2, 3, half_rows, heads, size), BF16), DMA((6,))],
        compiler_params=pltpu.CompilerParams(vmem_limit_bytes=16 * 2**20),
        cost_estimate=pl.CostEstimate(flops=WORK, bytes_accessed=2**16, transcendentals=0),
        name="query_sides",
    )(in_hbm(queries), in_hbm(grads), in_hbm(saved))


def shards(queries, key_heads, value_heads, forward_out, output_grad, block_order):
    _, tokens, groups, size = key_heads.shape
    q_heads = queries.shape[2]
    per_group = q_heads // groups
    per_stage = groups // STAGES
    pipe = lax.axis_size("pipe")
    blocks = lax.axis_size("ctx")
    keys = blocks * tokens
    rows = tokens // 2 * per_group
    packed = ((2, per_stage, tokens, size), BF16)
    flat = ((tokens * groups, size), BF16)
    rows_scratch = pltpu.VMEM(*flat[:1], F32)
    kv_parts = pl.pallas_call(
        functools.partial(prep_kernel, groups, per_stage),
        in_specs=[HBM] * 2,
        out_specs=[VMEM] * STAGES,
        out_shape=[jax.ShapeDtypeStruct(*packed)] * STAGES,
        scratch_shapes=[rows_scratch, pltpu.VMEM(*flat), pltpu.VMEM(*flat), DMA((2,))],
        compiler_params=pltpu.CompilerParams(vmem_limit_bytes=8 * 2**20),
        cost_estimate=pl.CostEstimate(flops=WORK, bytes_accessed=2**16, transcendentals=0),
        name="pack_keys",
    )(in_hbm(key_heads.reshape(-1, size)), in_hbm(value_heads.reshape(-1, size)))
    limit = 12 + keys // 64
    def sides_of(stage, grads):
        return make_sides(stage, STAGES, per_stage, queries[0], grads, forward_out[0])

    def key_sums(probs, dscore, sides):
        return call(
            dkv_kernel, "key_grads", [packed] * blocks, [], limit, WORK, [*sides, probs, dscore]
        )

    handed, sums = [], []
    block = kv_parts[0]
    up, down = passed(block, "ctx", 1), passed(block, "ctx", -1)
    sides = sides_of(0, output_grad[0])
    for stage in range(STAGES):
        if stage == 0:
            up, sides = lax.optimization_barrier((up, sides))
        else:
            up, down, _ = lax.optimization_barrier((up, down, handed_part))
            grads, probs, _ = lax.optimization_barrier((output_grad[0], probs, up))
            parts = key_sums(probs, dscore, sides)
            sides = sides_of(stage, grads)
        gathered = later_pass(block, up, down, "ctx")
        if stage > 0:
            parts, gathered = lax.optimization_barrier((parts, gathered))
            sums.append(scatter_sums(parts, "ctx"))
        if stage + 1 < STAGES:
            block, _ = lax.optimization_barrier((kv_parts[stage + 1], down))
            up, down = passed(block, "ctx", 1), passed(block, "ctx", -1)
        handed_part, probs, dscore = call(
            functools.partial(dq_kernel, blocks),
            "query_grads",
            [((tokens, per_stage * per_group, size), BF16)]
            + [((per_stage, keys, 2 * rows), BF16)] * 2,
            [
                pltpu.VMEM((2, keys, rows), F32),
                pltpu.VMEM((2, per_stage, keys, 2 * size), BF16),
                pltpu.VMEM((per_stage, keys, 2 * size), BF16),
                pltpu.VMEM((per_stage, 2 * size, keys), BF16),
            ],
            limit,
            DQ_WORK,
            [block_order, *sides, *gathered],
            True,
        )
        handed.append(
            lax.ppermute(handed_part, "pipe", [(place, place - 1) for place in range(1, pipe)])
        )
        if stage > 0:
            probs, _ = lax.optimization_barrier((probs, handed[stage - 1]))
    parts = key_sums(probs, dscore, sides)
    sums.append(scatter_sums(parts, "ctx"))
    key_grad, value_grad = call(
        functools.partial(finish_kernel, groups, per_stage, len(sums[0])),
        "lay_out",
        [flat, flat],
        [rows_scratch],
        8,
        WORK,
        [term for terms in sums for term in terms],
    )
    shape = key_heads.shape
    return (
        key_grad.reshape(shape),
        value_grad.reshape(shape),
        jnp.concatenate(handed, axis=1)[None],
    )


def solution(mesh):
    placed = P("pipe", "ctx", "head", None)
    return jax.shard_map(
        shards,
        mesh=mesh,
        in_specs=(placed,) * 5 + (P(),),
        out_specs=(placed,) * 3,
        check_vma=False,
    )
```

```python
import functools
import math

import jax
import jax.numpy as jnp
from jax import lax
from jax.experimental import pallas as pl
from jax.experimental.pallas import tpu as pltpu
from jax.sharding import PartitionSpec as P

NEG = -1e30
STAGES = 2
WORK = 2**20
BIG_WORK = 2**32
F32 = jnp.float32
BF16 = jnp.bfloat16


def signs(size):
    row = lax.broadcasted_iota(jnp.int32, (size, size), 0)
    col = lax.broadcasted_iota(jnp.int32, (size, size), 1)
    bits = row & col
    for step in (4, 2, 1):
        bits = bits ^ (bits >> step)
    return (1 - 2 * (bits & 1)).astype(F32).astype(BF16)


def dot(a, b, contract):
    return lax.dot_general(a, b, (contract, ((), ())), preferred_element_type=F32)


def nn(a, b):
    return dot(a, b, ((1,), (0,)))


def nt(a, b):
    return dot(a, b, ((1,), (1,)))


def split(x):
    high = x.astype(BF16)
    return high, (x - high.astype(F32)).astype(BF16)


def prep_kernel(k_hbm, v_hbm, k_out, v_out, rows_ref, k_ref, v_ref, sems):
    copies = [
        pltpu.make_async_copy(source, target, sems.at[at])
        for at, (source, target) in enumerate(((k_hbm, k_ref), (v_hbm, v_ref)))
    ]
    for copy in copies:
        copy.start()
    groups, tokens, size = k_out.shape
    sign = signs(size)
    for copy, ref, out in zip(copies, (k_ref, v_ref), (k_out, v_out)):
        copy.wait()
        if ref is k_ref:
            rows = nn(k_ref[...], sign) * (1.0 / math.sqrt(size))
        else:
            rows = v_ref[...].astype(F32)
        rows_ref[...] = rows
        for group in range(groups):
            out[group] = rows_ref[pl.ds(group, tokens, stride=groups), :].astype(BF16)


def finish_kernel(count, *refs):
    outs, rows_ref = refs[-3:-1], refs[-1]
    for part, out in enumerate(outs):
        terms = refs[part * count : (part + 1) * count]
        groups, tokens, _ = terms[0].shape
        for group in range(groups):
            rows = [ref[group].astype(F32) for ref in terms]
            rows_ref[pl.ds(group, tokens, stride=groups), :] = sum(rows[1:], rows[0])
        out[...] = rows_ref[...].astype(BF16)


def ring_order(count):
    return [0] + [at for at in range(count) if at % 2] + [at for at in range(count - 1, 0, -1) if at % 2 == 0]


def ring_place(count, place):
    odd = place & 1
    half = place >> 1
    return lax.rem(odd * (half + 1) + (1 - odd) * (count - half), count)


def ring_device(count, ring):
    return jnp.where(ring <= count // 2, jnp.maximum(2 * ring - 1, 0), 2 * (count - ring))


def passed(value, axis, step):
    count = lax.axis_size(axis)
    order = ring_order(count)
    return lax.ppermute(
        value, axis, [(order[at], order[(at + step) % count]) for at in range(count)]
    )


def gather(block, axis, relay_after=None):
    count = lax.axis_size(axis)
    blocks = {0: block}
    for step in range(1, count // 2 + 1):
        for sign in (1, -1):
            if sign < 0 and 2 * step == count:
                continue
            if step > 1 and relay_after is not None:
                moving, shift = blocks[(sign * (step - 1)) % count], sign
                if step == 2:
                    moving, _ = lax.optimization_barrier((moving, relay_after))
            else:
                moving, shift = block, sign * step
            blocks[(sign * step) % count] = passed(moving, axis, shift)
    return [blocks[step] for step in range(count)]


def passed_down(value, axis):
    count = lax.axis_size(axis)
    return lax.ppermute(value, axis, [(at, (at - 1) % count) for at in range(count)])


def added(a, b):
    return (a.astype(F32) + b.astype(F32)).astype(BF16)


def scatter_sums(parts, axis, relay_after):
    count = lax.axis_size(axis)
    terms, relayed = [parts[0]], []
    for step, longest in ((1, count // 2), (-1, (count - 1) // 2)):
        moving = None
        for distance in range(longest, 0, -1):
            part = parts[(-step * distance) % count]
            if moving is not None:
                moving, _ = lax.optimization_barrier((moving, relay_after))
                part = added(moving, part)
                relayed.append(part)
            moving = passed(part, axis, step)
        terms.append(moving)
    return terms, relayed


def sides_kernel(groups, q_hbm, g_hbm, o_hbm, q_side_ref, g_side_ref, in_ref, sems):
    _, _, half_rows, heads, size = in_ref.shape
    per_group = heads // groups
    copies = []
    for half in range(2):
        for part, source in enumerate((q_hbm, g_hbm, o_hbm)):
            piece = source.at[pl.ds(half * half_rows, half_rows)]
            copies.append(
                pltpu.make_async_copy(piece, in_ref.at[half, part], sems.at[half * 3 + part])
            )
            copies[-1].start()
    rows = half_rows * per_group
    sign = signs(size)
    root = 1.0 / math.sqrt(size)
    row_offset = lax.broadcasted_iota(jnp.int32, (rows, size), 0) // per_group
    lane = lax.broadcasted_iota(jnp.int32, (rows, size), 1)
    hide = jnp.where(row_offset == lane, NEG, 0.0).astype(BF16)
    for half in range(2):
        for copy in copies[3 * half : 3 * half + 3]:
            copy.wait()
        q_all = nn(in_ref[half, 0].reshape(half_rows * heads, size), sign) * root
        q_all = q_all.reshape(half_rows, groups, per_group, size)
        g_all = in_ref[half, 1].astype(F32).reshape(half_rows, groups, per_group, size)
        o_all = in_ref[half, 2].astype(F32).reshape(half_rows, groups, per_group, size)
        for group in range(groups):
            grad = g_all[:, group].reshape(rows, size)
            product = grad * o_all[:, group].reshape(rows, size)
            product = -(product + pltpu.roll(product, size // 2, 1))
            high = product.astype(BF16).astype(F32)
            delta = jnp.where(lane < size // 2, high, product - high)
            q_side_ref[half, group, :, :size] = q_all[:, group].reshape(rows, size).astype(BF16)
            q_side_ref[half, group, :, size:] = hide
            g_side_ref[half, group, :, :size] = grad.astype(BF16)
            g_side_ref[half, group, :, size:] = delta.astype(BF16)


def chunked(keys, chunk, body, init):
    if keys == chunk:
        return body(0, init)
    return lax.fori_loop(0, keys // chunk, body, init)


def weights_kernel(first, blocks, order_ref, q_side_ref, g_side_ref, *refs):
    k_refs, probs_ref, sum_refs = refs[:blocks], refs[blocks], refs[blocks + 1 : 2 * blocks + 1]
    score_ref, key_ref = refs[2 * blocks + 1 :]
    groups, keys, _ = probs_ref.shape
    tokens, size = k_refs[0].shape[1:]
    place = lax.axis_index("ctx")
    ring = ring_place(blocks, place)
    rows = q_side_ref.shape[2]
    half_rows = tokens // 2
    chunk = 512
    power = math.log2(math.e) / math.sqrt(size)

    def span(index):
        return pl.ds(pl.multiple_of(index * chunk, chunk), chunk)

    at_row = lax.broadcasted_iota(jnp.int32, (half_rows, size), 0)
    at_col = lax.broadcasted_iota(jnp.int32, (half_rows, size), 1)
    for block in range(blocks):
        source = ring_device(blocks, lax.rem(ring - block + blocks, blocks))
        for half in range(2):
            q_start = order_ref[place * 2 + half]
            for k_half in range(2):
                ahead = (order_ref[source * 2 + k_half] - q_start) * half_rows
                hidden = (at_row + ahead > at_col) & (at_col < half_rows)
                hidden = jnp.where(hidden, 1.0, 0.0).astype(BF16)
                k_at = pl.ds(block * tokens + k_half * half_rows, half_rows)
                for group in range(groups):
                    key_ref[half, group, k_at, size:] = hidden
        at = pl.ds(block * tokens, tokens)
        for group in range(groups):
            key = k_refs[block][first + group]
            for half in range(2):
                key_ref[half, group, at, :size] = key

    for group in range(groups):
        for half in range(2):
            q_side = q_side_ref.at[half, first + group]
            row_at = pl.ds(half * rows, rows)

            def scores(index, top, half=half, group=group, q_side=q_side):
                part = nt(key_ref[half, group, span(index), :], q_side[...])
                score_ref[half, span(index), :] = part
                return jnp.maximum(top, jnp.max(part.reshape(chunk // 8, 8, rows), axis=0))

            top = chunked(keys, chunk, scores, jnp.full((8, rows), NEG, F32))
            top = jnp.max(top, axis=0, keepdims=True)

            def weigh(index, total, half=half, top=top):
                part = jnp.exp2((score_ref[half, span(index), :] - top) * power)
                score_ref[half, span(index), :] = part
                return total + jnp.sum(part.reshape(chunk // 8, 8, rows), axis=0)

            total = chunked(keys, chunk, weigh, jnp.zeros((8, rows), F32))
            scale = 1.0 / jnp.sum(total, axis=0, keepdims=True)

            def settle(index, carried, half=half, group=group, scale=scale, row_at=row_at):
                probs = score_ref[half, span(index), :] * scale
                probs_ref[group, span(index), row_at] = probs.astype(probs_ref.dtype)
                return carried

            chunked(keys, chunk, settle, 0)
        for row in range(0, keys, chunk):
            dv = None
            for half in range(2):
                probs = probs_ref[group, pl.ds(row, chunk), pl.ds(half * rows, rows)]
                part = nn(probs.astype(BF16), g_side_ref[half, first + group, :, :size])
                dv = part if dv is None else dv + part
            dv = dv.astype(BF16)
            for at in range(0, chunk, tokens):
                sum_refs[(row + at) // tokens][group] = dv[at : at + tokens]


def dq_kernel(first, blocks, g_side_ref, probs_ref, *refs):
    k_refs, v_refs = refs[:blocks], refs[blocks : 2 * blocks]
    handed_ref, dscore_ref, val_ref, back_ref = refs[2 * blocks :]
    groups, keys, _ = probs_ref.shape
    tokens, size = k_refs[0].shape[1:]
    rows = g_side_ref.shape[2]
    half_rows = tokens // 2
    per_group = rows // half_rows
    chunk = 512
    sign = signs(size)

    def span(index):
        return pl.ds(pl.multiple_of(index * chunk, chunk), chunk)

    for block in range(blocks):
        at = pl.ds(block * tokens, tokens)
        for group in range(groups):
            val_ref[group, at, :size] = v_refs[block][first + group]
            val_ref[group, at, size:] = jnp.ones((tokens, size), BF16)
            high, low = split(nt(sign, k_refs[block][first + group]) * (1.0 / size))
            back_ref[group, :size, at] = high
            back_ref[group, size:, at] = low

    for half in range(2):
        results = []
        for group in range(groups):
            g_side = g_side_ref.at[half, first + group]
            row_at = pl.ds(half * rows, rows)

            def grads(index, dq, group=group, g_side=g_side, row_at=row_at):
                change = nt(val_ref[group, span(index), :], g_side[...])
                probs = probs_ref[group, span(index), row_at].astype(F32)
                dscore = (probs * change).astype(BF16)
                dscore_ref[group, span(index), row_at] = dscore
                return dq + nn(back_ref[group, :, span(index)], dscore)

            dq = chunked(keys, chunk, grads, jnp.zeros((2 * size, rows), F32))
            dq = (dq[:size] + dq[size:]).T + g_side[:, :size].astype(F32)
            results.append(dq.reshape(half_rows, per_group, size))
        at = pl.ds(half * half_rows, half_rows)
        handed_ref[at] = jnp.concatenate(results, axis=1).astype(BF16)


def dk_kernel(stages, q_side_ref, *refs):
    dscore_refs, sum_refs = refs[:stages], refs[stages:]
    tokens, size = sum_refs[0].shape[1:]
    rows = q_side_ref.shape[2]
    sign = signs(size)
    chunk = 512
    per_stage, keys, _ = dscore_refs[0].shape
    for row in range(0, keys, chunk):
        for group in range(stages * per_stage):
            dk = None
            for half in range(2):
                dscore = dscore_refs[group // per_stage].at[group % per_stage]
                dscore = dscore[pl.ds(row, chunk), pl.ds(half * rows, rows)]
                part = nn(dscore, q_side_ref[half, group, :, :size])
                dk = part if dk is None else dk + part
            high, low = split(dk)
            dk = ((nn(high, sign) + nn(low, sign)) * (1.0 / size)).astype(BF16)
            for at in range(0, chunk, tokens):
                sum_refs[(row + at) // tokens][group] = dk[at : at + tokens]


VMEM = pl.BlockSpec(memory_space=pltpu.VMEM)
HBM = pl.BlockSpec(memory_space=pltpu.HBM)
DMA = pltpu.SemaphoreType.DMA
SMEM = pl.BlockSpec(memory_space=pltpu.SMEM)


def call(kernel, name, outs, scratch, limit, work, args, smem=False):
    shapes = [jax.ShapeDtypeStruct(*out) for out in outs]
    return pl.pallas_call(
        kernel,
        in_specs=([SMEM] if smem else []) + [VMEM] * (len(args) - smem),
        out_specs=[VMEM] * len(outs),
        out_shape=shapes,
        scratch_shapes=scratch,
        compiler_params=pltpu.CompilerParams(vmem_limit_bytes=limit * 2**20),
        cost_estimate=pl.CostEstimate(flops=work, bytes_accessed=2**16, transcendentals=0),
        name=name,
    )(*args)


def in_hbm(value):
    return pltpu.with_memory_space_constraint(value, pltpu.HBM)


def make_sides(groups, queries, grads, saved):
    tokens, heads, size = queries.shape
    half_rows = tokens // 2
    rows = half_rows * heads // groups
    shape = jax.ShapeDtypeStruct((2, groups, rows, 2 * size), BF16)
    return pl.pallas_call(
        functools.partial(sides_kernel, groups),
        in_specs=[HBM] * 3,
        out_specs=[VMEM] * 2,
        out_shape=[shape] * 2,
        scratch_shapes=[pltpu.VMEM((2, 3, half_rows, heads, size), BF16), DMA((6,))],
        compiler_params=pltpu.CompilerParams(vmem_limit_bytes=24 * 2**20),
        cost_estimate=pl.CostEstimate(flops=WORK, bytes_accessed=2**16, transcendentals=0),
        name="query_sides",
    )(in_hbm(queries), in_hbm(grads), in_hbm(saved))


def shards(queries, key_heads, value_heads, forward_out, output_grad, block_order):
    _, tokens, groups, size = key_heads.shape
    q_heads = queries.shape[2]
    per_group = q_heads // groups
    per_stage = groups // STAGES
    blocks = lax.axis_size("ctx")
    keys = blocks * tokens
    rows = tokens // 2 * per_group
    probs_type = F32 if keys <= 1024 else BF16
    packed = ((groups, tokens, size), BF16)
    part = ((per_stage, tokens, size), BF16)
    flat = ((tokens * groups, size), BF16)
    rows_scratch = pltpu.VMEM(*flat[:1], F32)
    limit = 12 + keys // 64
    after = lax.optimization_barrier
    k_block, v_block = pl.pallas_call(
        prep_kernel,
        in_specs=[HBM] * 2,
        out_specs=[VMEM] * 2,
        out_shape=[jax.ShapeDtypeStruct(*packed)] * 2,
        scratch_shapes=[rows_scratch, pltpu.VMEM(*flat), pltpu.VMEM(*flat), DMA((2,))],
        compiler_params=pltpu.CompilerParams(vmem_limit_bytes=8 * 2**20),
        cost_estimate=pl.CostEstimate(flops=WORK, bytes_accessed=2**16, transcendentals=0),
        name="pack_keys",
    )(in_hbm(key_heads.reshape(-1, size)), in_hbm(value_heads.reshape(-1, size)))

    q_side, g_side = make_sides(groups, queries[0], output_grad[0], forward_out[0])
    k_all = gather(k_block, "ctx", (q_side, g_side))
    v_block, _ = after((v_block, (k_all[1], k_all[-1], q_side)))

    probs, dv_parts = [], []
    for stage in range(STAGES):
        stage_probs, *parts = call(
            functools.partial(weights_kernel, stage * per_stage, blocks),
            "weights",
            [((per_stage, keys, 2 * rows), probs_type)] + [part] * blocks,
            [
                pltpu.VMEM((2, keys, rows), F32),
                pltpu.VMEM((2, per_stage, keys, 2 * size), BF16),
            ],
            limit,
            BIG_WORK,
            [block_order, q_side, g_side, *k_all],
            True,
        )
        if stage == 0:
            v_all = gather(v_block, "ctx", stage_probs)
            q_side, _ = after((q_side, stage_probs))
        probs.append(stage_probs)
        dv_parts.append(parts)
    dv_parts = [jnp.concatenate(parts, axis=0) for parts in zip(*dv_parts)]

    handed, dscores = [], []
    for stage in range(STAGES):
        handed_part, dscore = call(
            functools.partial(dq_kernel, stage * per_stage, blocks),
            "query_grads",
            [((tokens, per_stage * per_group, size), BF16)]
            + [((per_stage, keys, 2 * rows), BF16)],
            [
                pltpu.VMEM((per_stage, keys, 2 * size), BF16),
                pltpu.VMEM((per_stage, 2 * size, keys), BF16),
            ],
            limit,
            BIG_WORK,
            [g_side, probs[stage], *k_all, *v_all],
        )
        if stage == 0:
            g_side, _ = after((g_side, handed_part))
        handed.append(passed_down(handed_part, "pipe"))
        dscores.append(dscore)
    dv_terms, dv_relayed = scatter_sums(dv_parts, "ctx", ())
    dscores, _ = after((dscores, (dv_relayed, dv_terms[-1])))
    dk_parts = call(
        functools.partial(dk_kernel, STAGES),
        "key_grads",
        [packed] * blocks,
        [],
        limit,
        WORK,
        [q_side, *dscores],
    )
    dk_terms, _ = scatter_sums(dk_parts, "ctx", ())
    key_grad, value_grad = call(
        functools.partial(finish_kernel, len(dk_terms)),
        "lay_out",
        [flat, flat],
        [rows_scratch],
        8,
        WORK,
        [*dk_terms, *dv_terms],
    )
    handed = jnp.concatenate(handed, axis=1)[None]
    last = lax.axis_index("pipe") == lax.axis_size("pipe") - 1
    shape = key_heads.shape
    return (
        key_grad.reshape(shape),
        value_grad.reshape(shape),
        jnp.where(last, jnp.zeros_like(handed), handed),
    )


def solution(mesh):
    placed = P("pipe", "ctx", "head", None)
    return jax.shard_map(
        shards,
        mesh=mesh,
        in_specs=(placed,) * 5 + (P(),),
        out_specs=(placed,) * 3,
        check_vma=False,
    )
```

```python
import functools
import math

import jax
import jax.numpy as jnp
from jax import lax
from jax.experimental import pallas as pl
from jax.experimental.pallas import tpu as pltpu
from jax.sharding import PartitionSpec as P

NEG = -1e30
STAGES = 2
WORK = 2**20
BIG_WORK = 2**32
F32 = jnp.float32
BF16 = jnp.bfloat16


def signs(size):
    row = lax.broadcasted_iota(jnp.int32, (size, size), 0)
    col = lax.broadcasted_iota(jnp.int32, (size, size), 1)
    bits = row & col
    for step in (4, 2, 1):
        bits = bits ^ (bits >> step)
    return (1 - 2 * (bits & 1)).astype(F32).astype(BF16)


def dot(a, b, contract):
    return lax.dot_general(a, b, (contract, ((), ())), preferred_element_type=F32)


def nn(a, b):
    return dot(a, b, ((1,), (0,)))


def nt(a, b):
    return dot(a, b, ((1,), (1,)))


def split(x):
    high = x.astype(BF16)
    return high, (x - high.astype(F32)).astype(BF16)


def prep_kernel(k_hbm, v_hbm, k_out, v_out, rows_ref, k_ref, v_ref, sems):
    copies = [
        pltpu.make_async_copy(source, target, sems.at[at])
        for at, (source, target) in enumerate(((k_hbm, k_ref), (v_hbm, v_ref)))
    ]
    for copy in copies:
        copy.start()
    groups, tokens, size = k_out.shape
    sign = signs(size)
    for copy, ref, out in zip(copies, (k_ref, v_ref), (k_out, v_out)):
        copy.wait()
        if ref is k_ref:
            rows = nn(k_ref[...], sign) * (1.0 / math.sqrt(size))
        else:
            rows = v_ref[...].astype(F32)
        rows_ref[...] = rows
        for group in range(groups):
            out[group] = rows_ref[pl.ds(group, tokens, stride=groups), :].astype(BF16)


def finish_kernel(count, *refs):
    outs, rows_ref = refs[-3:-1], refs[-1]
    for part, out in enumerate(outs):
        terms = refs[part * count : (part + 1) * count]
        groups, tokens, _ = terms[0].shape
        for group in range(groups):
            rows = [ref[group].astype(F32) for ref in terms]
            rows_ref[pl.ds(group, tokens, stride=groups), :] = sum(rows[1:], rows[0])
        out[...] = rows_ref[...].astype(BF16)


def ring_order(count):
    return [0] + [at for at in range(count) if at % 2] + [at for at in range(count - 1, 0, -1) if at % 2 == 0]


def ring_place(count, place):
    odd = place & 1
    half = place >> 1
    return lax.rem(odd * (half + 1) + (1 - odd) * (count - half), count)


def ring_device(count, ring):
    return jnp.where(ring <= count // 2, jnp.maximum(2 * ring - 1, 0), 2 * (count - ring))


def passed(value, axis, step):
    count = lax.axis_size(axis)
    order = ring_order(count)
    return lax.ppermute(
        value, axis, [(order[at], order[(at + step) % count]) for at in range(count)]
    )


def gather(block, axis, relay_after=None):
    count = lax.axis_size(axis)
    blocks = {0: block}
    for step in range(1, count // 2 + 1):
        for sign in (1, -1):
            if sign < 0 and 2 * step == count:
                continue
            if step > 1 and relay_after is not None:
                moving, shift = blocks[(sign * (step - 1)) % count], sign
                if step == 2:
                    moving, _ = lax.optimization_barrier((moving, relay_after))
            else:
                moving, shift = block, sign * step
            blocks[(sign * step) % count] = passed(moving, axis, shift)
    return [blocks[step] for step in range(count)]


def passed_down(value, axis):
    count = lax.axis_size(axis)
    return lax.ppermute(value, axis, [(at, (at - 1) % count) for at in range(count)])


def added(a, b):
    return (a.astype(F32) + b.astype(F32)).astype(BF16)


def scatter_sums(parts, axis, relay_after):
    count = lax.axis_size(axis)
    terms, relayed = [parts[0]], []
    for step, longest in ((1, count // 2), (-1, (count - 1) // 2)):
        moving = None
        for distance in range(longest, 0, -1):
            part = parts[(-step * distance) % count]
            if moving is not None:
                moving, _ = lax.optimization_barrier((moving, relay_after))
                part = added(moving, part)
                relayed.append(part)
            moving = passed(part, axis, step)
        terms.append(moving)
    return terms, relayed


def sides_kernel(groups, q_hbm, g_hbm, o_hbm, q_side_ref, g_side_ref, in_ref, sems):
    _, _, half_rows, heads, size = in_ref.shape
    per_group = heads // groups
    copies = []
    for half in range(2):
        for part, source in enumerate((q_hbm, g_hbm, o_hbm)):
            piece = source.at[pl.ds(half * half_rows, half_rows)]
            copies.append(
                pltpu.make_async_copy(piece, in_ref.at[half, part], sems.at[half * 3 + part])
            )
            copies[-1].start()
    rows = half_rows * per_group
    sign = signs(size)
    root = 1.0 / math.sqrt(size)
    row_offset = lax.broadcasted_iota(jnp.int32, (rows, size), 0) // per_group
    lane = lax.broadcasted_iota(jnp.int32, (rows, size), 1)
    hide = jnp.where(row_offset == lane, NEG, 0.0).astype(BF16)
    for half in range(2):
        for copy in copies[3 * half : 3 * half + 3]:
            copy.wait()
        q_all = nn(in_ref[half, 0].reshape(half_rows * heads, size), sign) * root
        q_all = q_all.reshape(half_rows, groups, per_group, size)
        g_all = in_ref[half, 1].astype(F32).reshape(half_rows, groups, per_group, size)
        o_all = in_ref[half, 2].astype(F32).reshape(half_rows, groups, per_group, size)
        for group in range(groups):
            grad = g_all[:, group].reshape(rows, size)
            product = grad * o_all[:, group].reshape(rows, size)
            product = -(product + pltpu.roll(product, size // 2, 1))
            high = product.astype(BF16).astype(F32)
            delta = jnp.where(lane < size // 2, high, product - high)
            q_side_ref[half, group, :, :size] = q_all[:, group].reshape(rows, size).astype(BF16)
            q_side_ref[half, group, :, size:] = hide
            g_side_ref[half, group, :, :size] = grad.astype(BF16)
            g_side_ref[half, group, :, size:] = delta.astype(BF16)


def far_last(count):
    return [step for step in range(count) if step != count // 2] + [count // 2]


def weights_kernel(first, blocks, order_ref, q_side_ref, g_side_ref, *refs):
    k_refs, (weight_ref, scale_ref) = refs[:blocks], refs[blocks : blocks + 2]
    sum_refs, key_ref = refs[blocks + 2 : 2 * blocks + 2], refs[-1]
    groups, keys, _ = weight_ref.shape
    tokens, size = k_refs[0].shape[1:]
    place = lax.axis_index("ctx")
    ring = ring_place(blocks, place)
    rows = q_side_ref.shape[2]
    half_rows = tokens // 2
    power = math.log2(math.e) / math.sqrt(size)

    at_row = lax.broadcasted_iota(jnp.int32, (half_rows, size), 0)
    at_col = lax.broadcasted_iota(jnp.int32, (half_rows, size), 1)
    for block, distance in enumerate(far_last(blocks)):
        source = ring_device(blocks, lax.rem(ring - distance + blocks, blocks))
        for half in range(2):
            q_start = order_ref[place * 2 + half]
            for k_half in range(2):
                ahead = (order_ref[source * 2 + k_half] - q_start) * half_rows
                hidden = (at_row + ahead > at_col) & (at_col < half_rows)
                hidden = jnp.where(hidden, 1.0, 0.0).astype(BF16)
                k_at = pl.ds(block * tokens + k_half * half_rows, half_rows)
                for group in range(groups):
                    key_ref[half, group, k_at, size:] = hidden
        at = pl.ds(block * tokens, tokens)
        for group in range(groups):
            key = k_refs[block][first + group]
            for half in range(2):
                key_ref[half, group, at, :size] = key

    chunk = 256
    units = [(group, half) for group in range(groups) for half in range(2)]
    tops, scales = {}, {}
    for step in range(len(units) + 1):
        top = total = None
        for row in range(0, keys, chunk):
            k_at = pl.ds(row, chunk)
            if step < len(units):
                group, half = units[step]
                part = nt(key_ref[half, group, k_at, :], q_side_ref[half, first + group])
                weight_ref[group, k_at, pl.ds(half * rows, rows)] = part
                part = jnp.max(part.reshape(chunk // 8, 8, rows), axis=0)
                top = part if top is None else jnp.maximum(top, part)
            if step > 0:
                group, half = units[step - 1]
                part = weight_ref[group, k_at, pl.ds(half * rows, rows)]
                part = jnp.exp2((part - tops[step - 1]) * power)
                weight_ref[group, k_at, pl.ds(half * rows, rows)] = part
                part = jnp.sum(part.reshape(chunk // 8, 8, rows), axis=0)
                total = part if total is None else total + part
        if step < len(units):
            tops[step] = jnp.max(top, axis=0, keepdims=True)
        if step > 0:
            group, half = units[step - 1]
            scale = 1.0 / jnp.sum(total, axis=0, keepdims=True)
            scale_ref[group, :, pl.ds(half * rows, rows)] = jnp.broadcast_to(scale, (8, rows))
            scales[half] = scale
        if step == 0 or units[step - 1][1] == 0:
            continue
        for row in range(0, keys, 512):
            dv = None
            for half in range(2):
                probs = weight_ref[group, pl.ds(row, 512), pl.ds(half * rows, rows)] * scales[half]
                part = nn(probs.astype(BF16), g_side_ref[half, first + group, :, :size])
                dv = part if dv is None else dv + part
            dv = dv.astype(BF16)
            for at in range(0, 512, tokens):
                sum_refs[(row + at) // tokens][group] = dv[at : at + tokens]


def dq_kernel(first, blocks, g_side_ref, weight_ref, scale_ref, *refs):
    k_refs, v_refs = refs[:blocks], refs[blocks : 2 * blocks]
    handed_ref, dscore_ref, val_ref, back_ref = refs[2 * blocks :]
    groups, keys, _ = weight_ref.shape
    tokens, size = k_refs[0].shape[1:]
    rows = g_side_ref.shape[2]
    half_rows = tokens // 2
    per_group = rows // half_rows
    chunk = 512
    sign = signs(size)

    for block in range(blocks):
        at = pl.ds(block * tokens, tokens)
        for group in range(groups):
            val_ref[group, at, :size] = v_refs[block][first + group]
            val_ref[group, at, size:] = jnp.ones((tokens, size), BF16)
            high, low = split(nt(sign, k_refs[block][first + group]) * (1.0 / size))
            back_ref[group, :size, at] = high
            back_ref[group, size:, at] = low

    def change(unit, row):
        half, group = unit
        return nt(val_ref[group, pl.ds(row, chunk), :], g_side_ref[half, first + group])

    units = [(half, group) for half in range(2) for group in range(groups)]
    steps = [(unit, row) for unit in units for row in range(0, keys, chunk)]
    ahead = change(*steps[0])
    results, dq = [], None
    for step, ((half, group), row) in enumerate(steps):
        now = ahead
        if step + 1 < len(steps):
            ahead = change(*steps[step + 1])
        k_at, row_at = pl.ds(row, chunk), pl.ds(half * rows, rows)
        probs = weight_ref[group, k_at, row_at] * scale_ref[group, :1, row_at]
        dscore = (probs * now).astype(BF16)
        dscore_ref[group, k_at, row_at] = dscore
        part = nn(back_ref[group, :, k_at], dscore)
        dq = part if dq is None else dq + part
        if row + chunk == keys:
            dq = (dq[:size] + dq[size:]).T + g_side_ref[half, first + group, :, :size].astype(F32)
            results.append(dq.reshape(half_rows, per_group, size))
            dq = None
        if len(results) == groups:
            at = pl.ds(half * half_rows, half_rows)
            handed_ref[at] = jnp.concatenate(results, axis=1).astype(BF16)
            results = []


def dk_kernel(stages, start, q_side_ref, *refs):
    dscore_refs, sum_refs = refs[:stages], refs[stages:]
    tokens, size = sum_refs[0].shape[1:]
    rows = q_side_ref.shape[2]
    signs_twice = jnp.concatenate([signs(size)] * 2, axis=0)
    chunk = 512
    per_stage = dscore_refs[0].shape[0]
    count = len(sum_refs) * tokens
    for row in range(0, count, chunk):
        length = min(chunk, count - row)
        for group in range(stages * per_stage):
            dk = None
            for half in range(2):
                dscore = dscore_refs[group // per_stage].at[group % per_stage]
                dscore = dscore[pl.ds(start * tokens + row, length), pl.ds(half * rows, rows)]
                part = nn(dscore, q_side_ref[half, group, :, :size])
                dk = part if dk is None else dk + part
            dk = (nn(jnp.concatenate(split(dk), axis=1), signs_twice) * (1.0 / size)).astype(BF16)
            for at in range(0, length, tokens):
                sum_refs[(row + at) // tokens][group] = dk[at : at + tokens]


VMEM = pl.BlockSpec(memory_space=pltpu.VMEM)
HBM = pl.BlockSpec(memory_space=pltpu.HBM)
DMA = pltpu.SemaphoreType.DMA
SMEM = pl.BlockSpec(memory_space=pltpu.SMEM)


def call(kernel, name, outs, scratch, limit, work, args, smem=False):
    shapes = [jax.ShapeDtypeStruct(*out) for out in outs]
    return pl.pallas_call(
        kernel,
        in_specs=([SMEM] if smem else []) + [VMEM] * (len(args) - smem),
        out_specs=[VMEM] * len(outs),
        out_shape=shapes,
        scratch_shapes=scratch,
        compiler_params=pltpu.CompilerParams(vmem_limit_bytes=limit * 2**20),
        cost_estimate=pl.CostEstimate(flops=work, bytes_accessed=2**16, transcendentals=0),
        name=name,
    )(*args)


def in_hbm(value):
    return pltpu.with_memory_space_constraint(value, pltpu.HBM)


def make_sides(groups, queries, grads, saved):
    tokens, heads, size = queries.shape
    half_rows = tokens // 2
    rows = half_rows * heads // groups
    shape = jax.ShapeDtypeStruct((2, groups, rows, 2 * size), BF16)
    return pl.pallas_call(
        functools.partial(sides_kernel, groups),
        in_specs=[HBM] * 3,
        out_specs=[VMEM] * 2,
        out_shape=[shape] * 2,
        scratch_shapes=[pltpu.VMEM((2, 3, half_rows, heads, size), BF16), DMA((6,))],
        compiler_params=pltpu.CompilerParams(vmem_limit_bytes=24 * 2**20),
        cost_estimate=pl.CostEstimate(flops=WORK, bytes_accessed=2**16, transcendentals=0),
        name="query_sides",
    )(in_hbm(queries), in_hbm(grads), in_hbm(saved))


def shards(queries, key_heads, value_heads, forward_out, output_grad, block_order):
    _, tokens, groups, size = key_heads.shape
    q_heads = queries.shape[2]
    per_group = q_heads // groups
    per_stage = groups // STAGES
    blocks = lax.axis_size("ctx")
    keys = blocks * tokens
    rows = tokens // 2 * per_group
    packed = ((groups, tokens, size), BF16)
    part = ((per_stage, tokens, size), BF16)
    flat = ((tokens * groups, size), BF16)
    rows_scratch = pltpu.VMEM(*flat[:1], F32)
    limit = 12 + keys // 64
    after = lax.optimization_barrier
    k_block, v_block = pl.pallas_call(
        prep_kernel,
        in_specs=[HBM] * 2,
        out_specs=[VMEM] * 2,
        out_shape=[jax.ShapeDtypeStruct(*packed)] * 2,
        scratch_shapes=[rows_scratch, pltpu.VMEM(*flat), pltpu.VMEM(*flat), DMA((2,))],
        compiler_params=pltpu.CompilerParams(vmem_limit_bytes=8 * 2**20),
        cost_estimate=pl.CostEstimate(flops=WORK, bytes_accessed=2**16, transcendentals=0),
        name="pack_keys",
    )(in_hbm(key_heads.reshape(-1, size)), in_hbm(value_heads.reshape(-1, size)))

    k_all = gather(k_block, "ctx", ())
    q_loads, _ = after((queries[0], k_all[1]))
    q_side, g_side = make_sides(groups, q_loads, output_grad[0], forward_out[0])
    v_block, _ = after((v_block, q_side))
    v_all = gather(v_block, "ctx")
    slots = far_last(blocks)
    k_all, v_all = [k_all[step] for step in slots], [v_all[step] for step in slots]

    weights, dv_parts = [], []
    for stage in range(STAGES):
        weight, scale, *parts = call(
            functools.partial(weights_kernel, stage * per_stage, blocks),
            "weights",
            [((per_stage, keys, 2 * rows), F32), ((per_stage, 8, 2 * rows), F32)] + [part] * blocks,
            [pltpu.VMEM((2, per_stage, keys, 2 * size), BF16)],
            limit,
            BIG_WORK,
            [block_order, q_side, g_side, *k_all],
            True,
        )
        if stage == 0:
            q_side, _ = after((q_side, scale))
        weights.append((weight, scale))
        dv_parts.append(parts)

    g_side, _ = after((g_side, weights[-1][1]))
    handed, dscores = [], []
    for stage in range(STAGES):
        handed_part, dscore = call(
            functools.partial(dq_kernel, stage * per_stage, blocks),
            "query_grads",
            [((tokens, per_stage * per_group, size), BF16)]
            + [((per_stage, keys, 2 * rows), BF16)],
            [
                pltpu.VMEM((per_stage, keys, 2 * size), BF16),
                pltpu.VMEM((per_stage, 2 * size, keys), BF16),
            ],
            limit,
            BIG_WORK,
            [g_side, *weights[stage], *k_all, *v_all],
        )
        if stage == 0:
            g_side, dv_parts, _ = after((g_side, dv_parts, handed_part))
        handed.append(passed_down(handed_part, "pipe"))
        dscores.append(dscore)
    dv_parts = [jnp.concatenate(parts, axis=0) for parts in zip(*dv_parts)]
    dv_parts = [dv_parts[slots.index(step)] for step in range(blocks)]
    dv_terms, dv_relayed = scatter_sums(dv_parts, "ctx", ())

    def key_sums(start, stop, dscores):
        return call(
            functools.partial(dk_kernel, STAGES, start),
            "key_grads",
            [packed] * (stop - start),
            [],
            limit,
            WORK,
            [q_side, *dscores],
        )

    far_parts = key_sums(blocks - 1, blocks, dscores)
    dscores, _ = after((dscores, (far_parts, dv_relayed, dv_terms[-1])))
    dk_parts = key_sums(0, blocks - 1, dscores) + far_parts
    dk_parts = [dk_parts[slots.index(step)] for step in range(blocks)]
    dk_terms, _ = scatter_sums(dk_parts, "ctx", (dk_parts[0], dv_terms[1]))
    handed = jnp.concatenate(handed, axis=1)[None]
    last = lax.axis_index("pipe") == lax.axis_size("pipe") - 1
    handed = jnp.where(last, jnp.zeros_like(handed), handed)
    dk_terms[0], _ = after((dk_terms[0], handed))
    key_grad, value_grad = call(
        functools.partial(finish_kernel, len(dk_terms)),
        "lay_out",
        [flat, flat],
        [rows_scratch],
        8,
        WORK,
        [*dk_terms, *dv_terms],
    )
    shape = key_heads.shape
    return (
        key_grad.reshape(shape),
        value_grad.reshape(shape),
        handed,
    )


def solution(mesh):
    placed = P("pipe", "ctx", "head", None)
    return jax.shard_map(
        shards,
        mesh=mesh,
        in_specs=(placed,) * 5 + (P(),),
        out_specs=(placed,) * 3,
        check_vma=False,
    )
```

```python
import functools
import math

import jax
import jax.numpy as jnp
from jax import lax
from jax.experimental import pallas as pl
from jax.experimental.pallas import tpu as pltpu
from jax.sharding import PartitionSpec as P

NEG = -1e30
STAGES = 2
WORK = 2**20
BIG_WORK = (2**32, 2**30)
F32 = jnp.float32
BF16 = jnp.bfloat16


def signs(size):
    row = lax.broadcasted_iota(jnp.int32, (size, size), 0)
    col = lax.broadcasted_iota(jnp.int32, (size, size), 1)
    bits = row & col
    for step in (4, 2, 1):
        bits = bits ^ (bits >> step)
    return (1 - 2 * (bits & 1)).astype(F32).astype(BF16)


def dot(a, b, contract):
    return lax.dot_general(a, b, (contract, ((), ())), preferred_element_type=F32)


def nn(a, b):
    return dot(a, b, ((1,), (0,)))


def nt(a, b):
    return dot(a, b, ((1,), (1,)))


def split(x):
    high = x.astype(BF16)
    return high, (x - high.astype(F32)).astype(BF16)


def prep_kernel(k_hbm, v_hbm, *refs):
    outs, (rows_ref, k_ref, v_ref, sems) = refs[:-4], refs[-4:]
    copies = [
        pltpu.make_async_copy(source, target, sems.at[at])
        for at, (source, target) in enumerate(((k_hbm, k_ref), (v_hbm, v_ref)))
    ]
    for copy in copies:
        copy.start()
    both, tokens, size = outs[0].shape
    per_stage = both // 2
    groups = per_stage * len(outs)
    sign = signs(size)
    for part, copy in enumerate(copies):
        copy.wait()
        if part == 0:
            rows = nn(k_ref[...], sign) * (1.0 / math.sqrt(size))
        else:
            rows = v_ref[...].astype(F32)
        rows_ref[...] = rows
        for group in range(groups):
            picked = rows_ref[pl.ds(group, tokens, stride=groups), :].astype(BF16)
            outs[group // per_stage][part * per_stage + group % per_stage] = picked


def finish_kernel(stages, *refs):
    parts, outs, rows_ref = refs[:-3], refs[-3:-1], refs[-1]
    terms = len(parts) // stages
    both, tokens, _ = parts[0].shape
    per_stage = both // 2
    groups = per_stage * stages
    for part, out in enumerate(outs):
        for group in range(groups):
            first = group // per_stage * terms
            at = part * per_stage + group % per_stage
            rows = [ref[at].astype(F32) for ref in parts[first : first + terms]]
            rows_ref[pl.ds(group, tokens, stride=groups), :] = sum(rows[1:], rows[0])
        out[...] = rows_ref[...].astype(BF16)


def ring_order(count):
    return [0] + [at for at in range(count) if at % 2] + [at for at in range(count - 1, 0, -1) if at % 2 == 0]


def ring_place(count, place):
    odd = place & 1
    half = place >> 1
    return lax.rem(odd * (half + 1) + (1 - odd) * (count - half), count)


def ring_device(count, ring):
    return jnp.where(ring <= count // 2, jnp.maximum(2 * ring - 1, 0), 2 * (count - ring))


def passed(value, axis, step):
    count = lax.axis_size(axis)
    order = ring_order(count)
    return lax.ppermute(
        value, axis, [(order[at], order[(at + step) % count]) for at in range(count)]
    )


def gather(block, axis, relay_after=None):
    count = lax.axis_size(axis)
    blocks = {0: block}
    for step in range(1, count // 2 + 1):
        for sign in (1, -1):
            if sign < 0 and 2 * step == count:
                continue
            if step > 1 and relay_after is not None:
                moving, shift = blocks[(sign * (step - 1)) % count], sign
                if step == 2:
                    moving, _ = lax.optimization_barrier((moving, relay_after))
            else:
                moving, shift = block, sign * step
            blocks[(sign * step) % count] = passed(moving, axis, shift)
    return [blocks[step] for step in range(count)]


def passed_down(value, axis):
    count = lax.axis_size(axis)
    return lax.ppermute(value, axis, [(at, (at - 1) % count) for at in range(count)])


def added(a, b):
    return (a.astype(F32) + b.astype(F32)).astype(BF16)


def scatter_sums(parts, axis, relay_after):
    count = lax.axis_size(axis)
    terms, relayed = [parts[0]], []
    for step, longest in ((1, count // 2), (-1, (count - 1) // 2)):
        moving = None
        for distance in range(longest, 0, -1):
            part = parts[(-step * distance) % count]
            if moving is not None:
                moving, _ = lax.optimization_barrier((moving, relay_after))
                part = added(moving, part)
                relayed.append(part)
            moving = passed(part, axis, step)
        terms.append(moving)
    return terms, relayed


def sides_kernel(groups, q_hbm, g_hbm, o_hbm, q_side_ref, g_side_ref, in_ref, sems):
    _, _, half_rows, heads, size = in_ref.shape
    per_group = heads // groups
    copies = []
    for half in range(2):
        for part, source in enumerate((q_hbm, g_hbm, o_hbm)):
            piece = source.at[pl.ds(half * half_rows, half_rows)]
            copies.append(
                pltpu.make_async_copy(piece, in_ref.at[half, part], sems.at[half * 3 + part])
            )
            copies[-1].start()
    rows = half_rows * per_group
    sign = signs(size)
    root = 1.0 / math.sqrt(size)
    row_offset = lax.broadcasted_iota(jnp.int32, (rows, size), 0) // per_group
    lane = lax.broadcasted_iota(jnp.int32, (rows, size), 1)
    hide = jnp.where(row_offset == lane, NEG, 0.0).astype(BF16)
    for half in range(2):
        for copy in copies[3 * half : 3 * half + 3]:
            copy.wait()
        q_all = nn(in_ref[half, 0].reshape(half_rows * heads, size), sign) * root
        q_all = q_all.reshape(half_rows, groups, per_group, size)
        g_all = in_ref[half, 1].astype(F32).reshape(half_rows, groups, per_group, size)
        o_all = in_ref[half, 2].astype(F32).reshape(half_rows, groups, per_group, size)
        for group in range(groups):
            grad = g_all[:, group].reshape(rows, size)
            product = grad * o_all[:, group].reshape(rows, size)
            product = -(product + pltpu.roll(product, size // 2, 1))
            high = product.astype(BF16).astype(F32)
            delta = jnp.where(lane < size // 2, high, product - high)
            q_side_ref[half, group, :, :size] = q_all[:, group].reshape(rows, size).astype(BF16)
            q_side_ref[half, group, :, size:] = hide
            g_side_ref[half, group, :, :size] = grad.astype(BF16)
            g_side_ref[half, group, :, size:] = delta.astype(BF16)


def far_last(count):
    return [step for step in range(count) if step != count // 2] + [count // 2]


def weights_kernel(first, blocks, order_ref, q_side_ref, g_side_ref, *refs):
    k_refs, (weight_ref, scale_ref) = refs[:blocks], refs[blocks : blocks + 2]
    sum_refs, key_ref = refs[blocks + 2 : 2 * blocks + 2], refs[-1]
    groups, keys, _ = weight_ref.shape
    tokens, size = k_refs[0].shape[1:]
    place = lax.axis_index("ctx")
    ring = ring_place(blocks, place)
    rows = q_side_ref.shape[2]
    half_rows = tokens // 2
    power = math.log2(math.e) / math.sqrt(size)

    at_row = lax.broadcasted_iota(jnp.int32, (half_rows, size), 0)
    at_col = lax.broadcasted_iota(jnp.int32, (half_rows, size), 1)
    for block, distance in enumerate(far_last(blocks)):
        source = ring_device(blocks, lax.rem(ring - distance + blocks, blocks))
        for half in range(2):
            q_start = order_ref[place * 2 + half]
            for k_half in range(2):
                ahead = (order_ref[source * 2 + k_half] - q_start) * half_rows
                hidden = (at_row + ahead > at_col) & (at_col < half_rows)
                hidden = jnp.where(hidden, 1.0, 0.0).astype(BF16)
                k_at = pl.ds(block * tokens + k_half * half_rows, half_rows)
                for group in range(groups):
                    key_ref[half, group, k_at, size:] = hidden
        at = pl.ds(block * tokens, tokens)
        for group in range(groups):
            key = k_refs[block][group]
            for half in range(2):
                key_ref[half, group, at, :size] = key

    chunk = 256
    units = [(group, half) for group in range(groups) for half in range(2)]
    tops, scales = {}, {}
    for step in range(len(units) + 1):
        top = total = None
        for row in range(0, keys, chunk):
            k_at = pl.ds(row, chunk)
            if step < len(units):
                group, half = units[step]
                part = nt(key_ref[half, group, k_at, :], q_side_ref[half, first + group])
                weight_ref[group, k_at, pl.ds(half * rows, rows)] = part
                part = jnp.max(part.reshape(chunk // 8, 8, rows), axis=0)
                top = part if top is None else jnp.maximum(top, part)
            if step > 0:
                group, half = units[step - 1]
                part = weight_ref[group, k_at, pl.ds(half * rows, rows)]
                part = jnp.exp2((part - tops[step - 1]) * power)
                weight_ref[group, k_at, pl.ds(half * rows, rows)] = part
                part = jnp.sum(part.reshape(chunk // 8, 8, rows), axis=0)
                total = part if total is None else total + part
        if step < len(units):
            tops[step] = jnp.max(top, axis=0, keepdims=True)
        if step > 0:
            group, half = units[step - 1]
            scale = 1.0 / jnp.sum(total, axis=0, keepdims=True)
            scale_ref[group, :, pl.ds(half * rows, rows)] = jnp.broadcast_to(scale, (8, rows))
            scales[half] = scale
        if step == 0 or units[step - 1][1] == 0:
            continue
        for row in range(0, keys, 512):
            dv = None
            for half in range(2):
                probs = weight_ref[group, pl.ds(row, 512), pl.ds(half * rows, rows)] * scales[half]
                part = nn(probs.astype(BF16), g_side_ref[half, first + group, :, :size])
                dv = part if dv is None else dv + part
            dv = dv.astype(BF16)
            for at in range(0, 512, tokens):
                sum_refs[(row + at) // tokens][group] = dv[at : at + tokens]


def dq_kernel(first, blocks, g_side_ref, weight_ref, scale_ref, *refs):
    kv_refs = refs[:blocks]
    handed_ref, dscore_ref, val_ref, back_ref = refs[blocks:]
    groups, keys, _ = weight_ref.shape
    tokens, size = kv_refs[0].shape[1:]
    rows = g_side_ref.shape[2]
    half_rows = tokens // 2
    per_group = rows // half_rows
    chunk = 512
    sign = signs(size)

    for block in range(blocks):
        at = pl.ds(block * tokens, tokens)
        for group in range(groups):
            val_ref[group, at, :size] = kv_refs[block][groups + group]
            val_ref[group, at, size:] = jnp.ones((tokens, size), BF16)
            high, low = split(nt(sign, kv_refs[block][group]) * (1.0 / size))
            back_ref[group, :size, at] = high
            back_ref[group, size:, at] = low

    def change(unit, row):
        half, group = unit
        return nt(val_ref[group, pl.ds(row, chunk), :], g_side_ref[half, first + group])

    units = [(half, group) for half in range(2) for group in range(groups)]
    steps = [(unit, row) for unit in units for row in range(0, keys, chunk)]
    ahead = change(*steps[0])
    results, dq = [], None
    for step, ((half, group), row) in enumerate(steps):
        now = ahead
        if step + 1 < len(steps):
            ahead = change(*steps[step + 1])
        k_at, row_at = pl.ds(row, chunk), pl.ds(half * rows, rows)
        probs = weight_ref[group, k_at, row_at] * scale_ref[group, :1, row_at]
        dscore = (probs * now).astype(BF16)
        dscore_ref[group, k_at, row_at] = dscore
        part = nn(back_ref[group, :, k_at], dscore)
        dq = part if dq is None else dq + part
        if row + chunk == keys:
            dq = (dq[:size] + dq[size:]).T + g_side_ref[half, first + group, :, :size].astype(F32)
            results.append(dq.reshape(half_rows, per_group, size))
            dq = None
        if len(results) == groups:
            at = pl.ds(half * half_rows, half_rows)
            handed_ref[at] = jnp.concatenate(results, axis=1).astype(BF16)
            results = []


def dk_kernel(first, q_side_ref, dscore_ref, *sum_refs):
    tokens, size = sum_refs[0].shape[1:]
    groups, keys, _ = dscore_ref.shape
    rows = q_side_ref.shape[2]
    signs_twice = jnp.concatenate([signs(size)] * 2, axis=0)
    for row in range(0, keys, 512):
        for group in range(groups):
            dk = None
            for half in range(2):
                dscore = dscore_ref[group, pl.ds(row, 512), pl.ds(half * rows, rows)]
                part = nn(dscore, q_side_ref[half, first + group, :, :size])
                dk = part if dk is None else dk + part
            dk = (nn(jnp.concatenate(split(dk), axis=1), signs_twice) * (1.0 / size)).astype(BF16)
            for at in range(0, 512, tokens):
                sum_refs[(row + at) // tokens][group] = dk[at : at + tokens]


VMEM = pl.BlockSpec(memory_space=pltpu.VMEM)
HBM = pl.BlockSpec(memory_space=pltpu.HBM)
DMA = pltpu.SemaphoreType.DMA
SMEM = pl.BlockSpec(memory_space=pltpu.SMEM)


def call(kernel, name, outs, scratch, limit, work, args, smem=False):
    shapes = [jax.ShapeDtypeStruct(*out) for out in outs]
    return pl.pallas_call(
        kernel,
        in_specs=([SMEM] if smem else []) + [VMEM] * (len(args) - smem),
        out_specs=[VMEM] * len(outs),
        out_shape=shapes,
        scratch_shapes=scratch,
        compiler_params=pltpu.CompilerParams(vmem_limit_bytes=limit * 2**20),
        cost_estimate=pl.CostEstimate(flops=work, bytes_accessed=2**16, transcendentals=0),
        name=name,
    )(*args)


def in_hbm(value):
    return pltpu.with_memory_space_constraint(value, pltpu.HBM)


def make_sides(groups, queries, grads, saved):
    tokens, heads, size = queries.shape
    half_rows = tokens // 2
    rows = half_rows * heads // groups
    shape = jax.ShapeDtypeStruct((2, groups, rows, 2 * size), BF16)
    return pl.pallas_call(
        functools.partial(sides_kernel, groups),
        in_specs=[HBM] * 3,
        out_specs=[VMEM] * 2,
        out_shape=[shape] * 2,
        scratch_shapes=[pltpu.VMEM((2, 3, half_rows, heads, size), BF16), DMA((6,))],
        compiler_params=pltpu.CompilerParams(vmem_limit_bytes=12 * 2**20),
        cost_estimate=pl.CostEstimate(flops=WORK, bytes_accessed=2**16, transcendentals=0),
        name="query_sides",
    )(in_hbm(queries), in_hbm(grads), in_hbm(saved))


def shards(queries, key_heads, value_heads, forward_out, output_grad, block_order):
    _, tokens, groups, size = key_heads.shape
    q_heads = queries.shape[2]
    per_group = q_heads // groups
    per_stage = groups // STAGES
    blocks = lax.axis_size("ctx")
    keys = blocks * tokens
    rows = tokens // 2 * per_group
    packed = ((2 * per_stage, tokens, size), BF16)
    part = ((per_stage, tokens, size), BF16)
    flat = ((tokens * groups, size), BF16)
    rows_scratch = pltpu.VMEM(*flat[:1], F32)
    limit = 6 + keys // 64
    after = lax.optimization_barrier
    slots = far_last(blocks)
    kv_blocks = pl.pallas_call(
        prep_kernel,
        in_specs=[HBM] * 2,
        out_specs=[VMEM] * STAGES,
        out_shape=[jax.ShapeDtypeStruct(*packed)] * STAGES,
        scratch_shapes=[rows_scratch, pltpu.VMEM(*flat), pltpu.VMEM(*flat), DMA((2,))],
        compiler_params=pltpu.CompilerParams(vmem_limit_bytes=8 * 2**20),
        cost_estimate=pl.CostEstimate(flops=WORK, bytes_accessed=2**16, transcendentals=0),
        name="pack_keys",
    )(in_hbm(key_heads.reshape(-1, size)), in_hbm(value_heads.reshape(-1, size)))

    gathered = [gather(kv_blocks[0], "ctx", ())]
    q_loads, _ = after((queries[0], gathered[0][1]))
    q_side, g_side = make_sides(groups, q_loads, output_grad[0], forward_out[0])
    for stage in range(1, STAGES):
        block, _ = after((kv_blocks[stage], q_side))
        gathered.append(gather(block, "ctx"))

    def sums_of(stage, dscore, dv_parts):
        dk_parts = call(
            functools.partial(dk_kernel, stage * per_stage),
            "key_grads",
            [part] * blocks,
            [],
            limit,
            WORK,
            [q_side, dscore],
        )
        parts = [jnp.concatenate(pair, axis=0) for pair in zip(dk_parts, dv_parts)]
        return [parts[slots.index(step)] for step in range(blocks)]

    handed, terms = [], []
    for stage in range(STAGES):
        kv_all = [gathered[stage][step] for step in slots]
        weight, scale, *dv_parts = call(
            functools.partial(weights_kernel, stage * per_stage, blocks),
            "weights",
            [((per_stage, keys, 2 * rows), F32), ((per_stage, 8, 2 * rows), F32)] + [part] * blocks,
            [pltpu.VMEM((2, per_stage, keys, 2 * size), BF16)],
            limit,
            BIG_WORK[min(stage, 1)],
            [block_order, q_side, g_side, *kv_all],
            True,
        )
        handed_part, dscore = call(
            functools.partial(dq_kernel, stage * per_stage, blocks),
            "query_grads",
            [((tokens, per_stage * per_group, size), BF16)]
            + [((per_stage, keys, 2 * rows), BF16)],
            [
                pltpu.VMEM((per_stage, keys, 2 * size), BF16),
                pltpu.VMEM((per_stage, 2 * size, keys), BF16),
            ],
            limit,
            BIG_WORK[min(stage, 1)],
            [g_side, weight, scale, *kv_all],
        )
        handed.append(passed_down(handed_part, "pipe"))
        if stage > 0:
            dscore, _ = after((dscore, (relayed, terms[-1], handed[0])))
        parts = sums_of(stage, dscore, dv_parts)
        q_side, _ = after((q_side, parts))
        stage_terms, relayed = scatter_sums(parts, "ctx", handed[:stage])
        terms += stage_terms
    key_grad, value_grad = call(
        functools.partial(finish_kernel, STAGES), "lay_out", [flat, flat], [rows_scratch], 8, WORK, terms
    )
    handed = jnp.concatenate(handed, axis=1)[None]
    last = lax.axis_index("pipe") == lax.axis_size("pipe") - 1
    handed = jnp.where(last, jnp.zeros_like(handed), handed)
    shape = key_heads.shape
    return (
        key_grad.reshape(shape),
        value_grad.reshape(shape),
        handed,
    )


def solution(mesh):
    placed = P("pipe", "ctx", "head", None)
    return jax.shard_map(
        shards,
        mesh=mesh,
        in_specs=(placed,) * 5 + (P(),),
        out_specs=(placed,) * 3,
        check_vma=False,
    )
```

```python
import functools
import math

import jax
import jax.numpy as jnp
from jax import lax
from jax.experimental import pallas as pl
from jax.experimental.pallas import tpu as pltpu
from jax.sharding import PartitionSpec as P

NEG = -1e30
STAGES = 2
WORK = 2**20
BIG_WORK = (2**32, 2**32, 2**32)
F32 = jnp.float32
BF16 = jnp.bfloat16


def signs(size):
    row = lax.broadcasted_iota(jnp.int32, (size, size), 0)
    col = lax.broadcasted_iota(jnp.int32, (size, size), 1)
    bits = row & col
    for step in (4, 2, 1):
        bits = bits ^ (bits >> step)
    return (1 - 2 * (bits & 1)).astype(F32).astype(BF16)


def dot(a, b, contract):
    return lax.dot_general(a, b, (contract, ((), ())), preferred_element_type=F32)


def nn(a, b):
    return dot(a, b, ((1,), (0,)))


def nt(a, b):
    return dot(a, b, ((1,), (1,)))


def split(x):
    high = x.astype(BF16)
    return high, (x - high.astype(F32)).astype(BF16)


def prep_kernel(k_hbm, v_hbm, *refs):
    outs, (rows_ref, k_ref, v_ref, sems) = refs[:-4], refs[-4:]
    copies = [
        pltpu.make_async_copy(source, target, sems.at[at])
        for at, (source, target) in enumerate(((k_hbm, k_ref), (v_hbm, v_ref)))
    ]
    for copy in copies:
        copy.start()
    both, tokens, size = outs[0].shape
    per_stage = both // 2
    groups = per_stage * len(outs)
    sign = signs(size)
    for part, copy in enumerate(copies):
        copy.wait()
        if part == 0:
            rows = nn(k_ref[...], sign) * (1.0 / math.sqrt(size))
        else:
            rows = v_ref[...].astype(F32)
        rows_ref[...] = rows
        for group in range(groups):
            picked = rows_ref[pl.ds(group, tokens, stride=groups), :].astype(BF16)
            outs[group // per_stage][part * per_stage + group % per_stage] = picked


def finish_kernel(counts, *refs):
    parts, outs, rows_ref = refs[:-3], refs[-3:-1], refs[-1]
    both, tokens, _ = parts[0].shape
    per_stage = both // 2
    groups = per_stage * len(counts)
    for part, out in enumerate(outs):
        for group in range(groups):
            stage = group // per_stage
            terms = parts[sum(counts[:stage]) : sum(counts[: stage + 1])]
            at = part * per_stage + group % per_stage
            rows = [ref[at].astype(F32) for ref in terms]
            rows_ref[pl.ds(group, tokens, stride=groups), :] = sum(rows[1:], rows[0])
        out[...] = rows_ref[...].astype(BF16)


def ring_order(count):
    return [0] + [at for at in range(count) if at % 2] + [at for at in range(count - 1, 0, -1) if at % 2 == 0]


def ring_place(count, place):
    odd = place & 1
    half = place >> 1
    return lax.rem(odd * (half + 1) + (1 - odd) * (count - half), count)


def ring_device(count, ring):
    return jnp.where(ring <= count // 2, jnp.maximum(2 * ring - 1, 0), 2 * (count - ring))


def passed(value, axis, step):
    count = lax.axis_size(axis)
    order = ring_order(count)
    return lax.ppermute(
        value, axis, [(order[at], order[(at + step) % count]) for at in range(count)]
    )


def gather_rest(block, up, down, axis):
    count = lax.axis_size(axis)
    blocks = {0: block, 1: up, count - 1: down}
    for step in range(2, count // 2 + 1):
        up = blocks[step] = passed(up, axis, 1)
        if 2 * step < count:
            down = blocks[count - step] = passed(down, axis, -1)
    return [blocks[step] for step in range(count)]


def passed_down(value, axis):
    count = lax.axis_size(axis)
    return lax.ppermute(value, axis, [(at, (at - 1) % count) for at in range(count)])


def added(a, b):
    return (a.astype(F32) + b.astype(F32)).astype(BF16)


def up_sums(parts, axis, joined=None, relay_after=()):
    count = lax.axis_size(axis)
    longest = count // 2
    part = parts[count - longest]
    arrived = None
    for distance in range(longest - 1, 0, -1):
        if arrived is None and joined is not None:
            both = passed(jnp.concatenate([joined, part], axis=0), axis, 1)
            arrived, moving = both[: joined.shape[0]], both[joined.shape[0] :]
        else:
            moving = passed(part, axis, 1)
        moving, _ = lax.optimization_barrier((moving, relay_after))
        part = added(moving, parts[count - distance])
    return part, arrived


def down_sums(parts, axis):
    count = lax.axis_size(axis)
    moving = None
    for distance in range((count - 1) // 2, 0, -1):
        part = parts[distance]
        moving = passed(part if moving is None else added(moving, part), axis, -1)
    return moving


def sides_kernel(groups, q_hbm, g_hbm, o_hbm, q_side_ref, g_side_ref, in_ref, sems):
    _, _, half_rows, heads, size = in_ref.shape
    per_group = heads // groups
    copies = []
    for half in range(2):
        for part, source in enumerate((q_hbm, g_hbm, o_hbm)):
            piece = source.at[pl.ds(half * half_rows, half_rows)]
            copies.append(
                pltpu.make_async_copy(piece, in_ref.at[half, part], sems.at[half * 3 + part])
            )
            copies[-1].start()
    rows = half_rows * per_group
    sign = signs(size)
    root = 1.0 / math.sqrt(size)
    row_offset = lax.broadcasted_iota(jnp.int32, (rows, size), 0) // per_group
    lane = lax.broadcasted_iota(jnp.int32, (rows, size), 1)
    hide = jnp.where(row_offset == lane, NEG, 0.0).astype(BF16)
    for half in range(2):
        for copy in copies[3 * half : 3 * half + 3]:
            copy.wait()
        q_all = nn(in_ref[half, 0].reshape(half_rows * heads, size), sign) * root
        q_all = q_all.reshape(half_rows, groups, per_group, size)
        g_all = in_ref[half, 1].astype(F32).reshape(half_rows, groups, per_group, size)
        o_all = in_ref[half, 2].astype(F32).reshape(half_rows, groups, per_group, size)
        for group in range(groups):
            grad = g_all[:, group].reshape(rows, size)
            product = grad * o_all[:, group].reshape(rows, size)
            product = -(product + pltpu.roll(product, size // 2, 1))
            high = product.astype(BF16).astype(F32)
            delta = jnp.where(lane < size // 2, high, product - high)
            q_side_ref[half, group, :, :size] = q_all[:, group].reshape(rows, size).astype(BF16)
            q_side_ref[half, group, :, size:] = hide
            g_side_ref[half, group, :, :size] = grad.astype(BF16)
            g_side_ref[half, group, :, size:] = delta.astype(BF16)


def far_last(count):
    return [step for step in range(count) if step != count // 2] + [count // 2]


def weights_kernel(first, blocks, order_ref, q_side_ref, g_side_ref, *refs):
    k_refs, (weight_ref, scale_ref) = refs[:blocks], refs[blocks : blocks + 2]
    sum_refs, key_ref = refs[blocks + 2 : 2 * blocks + 2], refs[-1]
    groups, keys, _ = weight_ref.shape
    tokens, size = k_refs[0].shape[1:]
    place = lax.axis_index("ctx")
    ring = ring_place(blocks, place)
    rows = q_side_ref.shape[2]
    half_rows = tokens // 2
    power = math.log2(math.e) / math.sqrt(size)

    at_row = lax.broadcasted_iota(jnp.int32, (half_rows, size), 0)
    at_col = lax.broadcasted_iota(jnp.int32, (half_rows, size), 1)
    for block, distance in enumerate(far_last(blocks)):
        source = ring_device(blocks, lax.rem(ring - distance + blocks, blocks))
        for half in range(2):
            q_start = order_ref[place * 2 + half]
            for k_half in range(2):
                ahead = (order_ref[source * 2 + k_half] - q_start) * half_rows
                hidden = (at_row + ahead > at_col) & (at_col < half_rows)
                hidden = jnp.where(hidden, 1.0, 0.0).astype(BF16)
                k_at = pl.ds(block * tokens + k_half * half_rows, half_rows)
                for group in range(groups):
                    key_ref[half, group, k_at, size:] = hidden
        at = pl.ds(block * tokens, tokens)
        for group in range(groups):
            key = k_refs[block][group]
            for half in range(2):
                key_ref[half, group, at, :size] = key

    chunk = 256
    units = [(group, half) for group in range(groups) for half in range(2)]
    tops, scales = {}, {}
    for step in range(len(units) + 1):
        top = total = None
        for row in range(0, keys, chunk):
            k_at = pl.ds(row, chunk)
            if step < len(units):
                group, half = units[step]
                part = nt(key_ref[half, group, k_at, :], q_side_ref[half, first + group])
                weight_ref[group, k_at, pl.ds(half * rows, rows)] = part
                part = jnp.max(part.reshape(chunk // 8, 8, rows), axis=0)
                top = part if top is None else jnp.maximum(top, part)
            if step > 0:
                group, half = units[step - 1]
                part = weight_ref[group, k_at, pl.ds(half * rows, rows)]
                part = jnp.exp2((part - tops[step - 1]) * power)
                weight_ref[group, k_at, pl.ds(half * rows, rows)] = part
                part = jnp.sum(part.reshape(chunk // 8, 8, rows), axis=0)
                total = part if total is None else total + part
        if step < len(units):
            tops[step] = jnp.max(top, axis=0, keepdims=True)
        if step > 0:
            group, half = units[step - 1]
            scale = 1.0 / jnp.sum(total, axis=0, keepdims=True)
            scale_ref[group, :, pl.ds(half * rows, rows)] = jnp.broadcast_to(scale, (8, rows))
            scales[half] = scale
        if step == 0 or units[step - 1][1] == 0:
            continue
        for row in range(0, keys, 512):
            dv = None
            for half in range(2):
                probs = weight_ref[group, pl.ds(row, 512), pl.ds(half * rows, rows)] * scales[half]
                part = nn(probs.astype(BF16), g_side_ref[half, first + group, :, :size])
                dv = part if dv is None else dv + part
            dv = dv.astype(BF16)
            for at in range(0, 512, tokens):
                sum_refs[(row + at) // tokens][group] = dv[at : at + tokens]


def dq_kernel(first, blocks, g_side_ref, weight_ref, scale_ref, *refs):
    kv_refs = refs[:blocks]
    handed_ref, dscore_ref, val_ref, back_ref = refs[blocks:]
    groups, keys, _ = weight_ref.shape
    tokens, size = kv_refs[0].shape[1:]
    rows = g_side_ref.shape[2]
    half_rows = tokens // 2
    per_group = rows // half_rows
    chunk = 512
    sign = signs(size)

    for block in range(blocks):
        at = pl.ds(block * tokens, tokens)
        for group in range(groups):
            val_ref[group, at, :size] = kv_refs[block][groups + group]
            val_ref[group, at, size:] = jnp.ones((tokens, size), BF16)
            high, low = split(nt(sign, kv_refs[block][group]) * (1.0 / size))
            back_ref[group, :size, at] = high
            back_ref[group, size:, at] = low

    def change(unit, row):
        half, group = unit
        return nt(val_ref[group, pl.ds(row, chunk), :], g_side_ref[half, first + group])

    units = [(half, group) for half in range(2) for group in range(groups)]
    steps = [(unit, row) for unit in units for row in range(0, keys, chunk)]
    ahead = change(*steps[0])
    results, dq = [], None
    for step, ((half, group), row) in enumerate(steps):
        now = ahead
        if step + 1 < len(steps):
            ahead = change(*steps[step + 1])
        k_at, row_at = pl.ds(row, chunk), pl.ds(half * rows, rows)
        probs = weight_ref[group, k_at, row_at] * scale_ref[group, :1, row_at]
        dscore = (probs * now).astype(BF16)
        dscore_ref[group, k_at, row_at] = dscore
        part = nn(back_ref[group, :, k_at], dscore)
        dq = part if dq is None else dq + part
        if row + chunk == keys:
            dq = (dq[:size] + dq[size:]).T + g_side_ref[half, first + group, :, :size].astype(F32)
            results.append(dq.reshape(half_rows, per_group, size))
            dq = None
        if len(results) == groups:
            at = pl.ds(half * half_rows, half_rows)
            handed_ref[at] = jnp.concatenate(results, axis=1).astype(BF16)
            results = []


def dk_kernel(first, q_side_ref, dscore_ref, *sum_refs):
    tokens, size = sum_refs[0].shape[1:]
    groups, keys, _ = dscore_ref.shape
    rows = q_side_ref.shape[2]
    signs_twice = jnp.concatenate([signs(size)] * 2, axis=0)
    for row in range(0, keys, 512):
        for group in range(groups):
            dk = None
            for half in range(2):
                dscore = dscore_ref[group, pl.ds(row, 512), pl.ds(half * rows, rows)]
                part = nn(dscore, q_side_ref[half, first + group, :, :size])
                dk = part if dk is None else dk + part
            dk = (nn(jnp.concatenate(split(dk), axis=1), signs_twice) * (1.0 / size)).astype(BF16)
            for at in range(0, 512, tokens):
                sum_refs[(row + at) // tokens][group] = dk[at : at + tokens]


VMEM = pl.BlockSpec(memory_space=pltpu.VMEM)
HBM = pl.BlockSpec(memory_space=pltpu.HBM)
DMA = pltpu.SemaphoreType.DMA
SMEM = pl.BlockSpec(memory_space=pltpu.SMEM)


def call(kernel, name, outs, scratch, limit, work, args, smem=False):
    shapes = [jax.ShapeDtypeStruct(*out) for out in outs]
    return pl.pallas_call(
        kernel,
        in_specs=([SMEM] if smem else []) + [VMEM] * (len(args) - smem),
        out_specs=[VMEM] * len(outs),
        out_shape=shapes,
        scratch_shapes=scratch,
        compiler_params=pltpu.CompilerParams(vmem_limit_bytes=limit * 2**20),
        cost_estimate=pl.CostEstimate(flops=work, bytes_accessed=2**16, transcendentals=0),
        name=name,
    )(*args)


def in_hbm(value):
    return pltpu.with_memory_space_constraint(value, pltpu.HBM)


def make_sides(groups, queries, grads, saved):
    tokens, heads, size = queries.shape
    half_rows = tokens // 2
    rows = half_rows * heads // groups
    shape = jax.ShapeDtypeStruct((2, groups, rows, 2 * size), BF16)
    return pl.pallas_call(
        functools.partial(sides_kernel, groups),
        in_specs=[HBM] * 3,
        out_specs=[VMEM] * 2,
        out_shape=[shape] * 2,
        scratch_shapes=[pltpu.VMEM((2, 3, half_rows, heads, size), BF16), DMA((6,))],
        compiler_params=pltpu.CompilerParams(vmem_limit_bytes=12 * 2**20),
        cost_estimate=pl.CostEstimate(flops=WORK, bytes_accessed=2**16, transcendentals=0),
        name="query_sides",
    )(in_hbm(queries), in_hbm(grads), in_hbm(saved))


def shards(queries, key_heads, value_heads, forward_out, output_grad, block_order):
    _, tokens, groups, size = key_heads.shape
    q_heads = queries.shape[2]
    per_group = q_heads // groups
    per_stage = groups // STAGES
    blocks = lax.axis_size("ctx")
    keys = blocks * tokens
    rows = tokens // 2 * per_group
    packed = ((2 * per_stage, tokens, size), BF16)
    part = ((per_stage, tokens, size), BF16)
    flat = ((tokens * groups, size), BF16)
    rows_scratch = pltpu.VMEM(*flat[:1], F32)
    limit = 6 + keys // 64
    after = lax.optimization_barrier
    slots = far_last(blocks)
    kv_blocks = pl.pallas_call(
        prep_kernel,
        in_specs=[HBM] * 2,
        out_specs=[VMEM] * STAGES,
        out_shape=[jax.ShapeDtypeStruct(*packed)] * STAGES,
        scratch_shapes=[rows_scratch, pltpu.VMEM(*flat), pltpu.VMEM(*flat), DMA((2,))],
        compiler_params=pltpu.CompilerParams(vmem_limit_bytes=8 * 2**20),
        cost_estimate=pl.CostEstimate(flops=WORK, bytes_accessed=2**16, transcendentals=0),
        name="pack_keys",
    )(in_hbm(key_heads.reshape(-1, size)), in_hbm(value_heads.reshape(-1, size)))

    near = [(passed(kv_blocks[0], "ctx", 1), passed(kv_blocks[0], "ctx", -1))]
    q_loads, _ = after((queries[0], near[0][0]))
    q_side, g_side = make_sides(groups, q_loads, output_grad[0], forward_out[0])
    for stage in range(1, STAGES):
        block, _ = after((kv_blocks[stage], q_side))
        near.append((passed(block, "ctx", 1), passed(block, "ctx", -1)))

    def sums_of(stage, dscore, dv_parts):
        dk_parts = call(
            functools.partial(dk_kernel, stage * per_stage),
            "key_grads",
            [part] * blocks,
            [],
            limit,
            WORK,
            [q_side, dscore],
        )
        parts = [jnp.concatenate(pair, axis=0) for pair in zip(dk_parts, dv_parts)]
        return [parts[slots.index(step)] for step in range(blocks)]

    handed, terms = [], []
    gathered = gather_rest(kv_blocks[0], *near[0], "ctx")
    last_hop = None
    for stage in range(STAGES):
        kv_all = [gathered[step] for step in slots]
        weight, scale, *dv_parts = call(
            functools.partial(weights_kernel, stage * per_stage, blocks),
            "weights",
            [((per_stage, keys, 2 * rows), F32), ((per_stage, 8, 2 * rows), F32)] + [part] * blocks,
            [pltpu.VMEM((2, per_stage, keys, 2 * size), BF16)],
            limit,
            BIG_WORK[min(stage, 1)],
            [block_order, q_side, g_side, *kv_all],
            True,
        )
        if stage + 1 < STAGES:
            up, down = near[stage + 1]
            up, scale = after((up, scale))
            gathered = gather_rest(kv_blocks[stage + 1], up, down, "ctx")
        handed_part, dscore = call(
            functools.partial(dq_kernel, stage * per_stage, blocks),
            "query_grads",
            [((tokens, per_stage * per_group, size), BF16)]
            + [((per_stage, keys, 2 * rows), BF16)],
            [
                pltpu.VMEM((per_stage, keys, 2 * size), BF16),
                pltpu.VMEM((per_stage, 2 * size, keys), BF16),
            ],
            limit,
            BIG_WORK[2 * min(stage, 1)],
            [g_side, weight, scale, *kv_all],
        )
        if stage == 0:
            handed.append(passed_down(handed_part, "pipe"))
        else:
            dscore, _ = after((dscore, (last_hop, terms[-1])))
        parts = sums_of(stage, dscore, dv_parts)
        q_side, _ = after((q_side, parts))
        if stage > 0:
            handed_part, _ = after((handed_part, parts))
            handed.append(passed_down(handed_part, "pipe"))
        last_hop, arrived = up_sums(parts, "ctx", last_hop, handed[:stage])
        if arrived is not None:
            terms[-1] = terms[-1] + [arrived]
        terms.append([parts[0], down_sums(parts, "ctx")])
    terms[-1].append(passed(last_hop, "ctx", 1))
    handed = jnp.concatenate(handed, axis=1)[None]
    last = lax.axis_index("pipe") == lax.axis_size("pipe") - 1
    handed = jnp.where(last, jnp.zeros_like(handed), handed)
    terms[0][0], _ = after((terms[0][0], handed))
    key_grad, value_grad = call(
        functools.partial(finish_kernel, [len(found) for found in terms]),
        "lay_out",
        [flat, flat],
        [rows_scratch],
        8,
        WORK,
        sum(terms, []),
    )
    shape = key_heads.shape
    return (
        key_grad.reshape(shape),
        value_grad.reshape(shape),
        handed,
    )


def solution(mesh):
    placed = P("pipe", "ctx", "head", None)
    return jax.shard_map(
        shards,
        mesh=mesh,
        in_specs=(placed,) * 5 + (P(),),
        out_specs=(placed,) * 3,
        check_vma=False,
    )
```

```python
import functools
import math

import jax
import jax.numpy as jnp
from jax import lax
from jax.experimental import pallas as pl
from jax.experimental.pallas import tpu as pltpu
from jax.sharding import PartitionSpec as P

NEG = -1e30
STAGES = 2
WORK = 2**20
BIG_WORK = 2**32
F32 = jnp.float32
BF16 = jnp.bfloat16


def signs(size):
    row = lax.broadcasted_iota(jnp.int32, (size, size), 0)
    col = lax.broadcasted_iota(jnp.int32, (size, size), 1)
    bits = row & col
    for step in (4, 2, 1):
        bits = bits ^ (bits >> step)
    return (1 - 2 * (bits & 1)).astype(F32).astype(BF16)


def dot(a, b, contract):
    return lax.dot_general(a, b, (contract, ((), ())), preferred_element_type=F32)


def nn(a, b):
    return dot(a, b, ((1,), (0,)))


def nt(a, b):
    return dot(a, b, ((1,), (1,)))


def split(x):
    high = x.astype(BF16)
    return high, (x - high.astype(F32)).astype(BF16)


def prep_kernel(k_hbm, v_hbm, k_out, v_out, rows_ref, k_ref, v_ref, sems):
    copies = [
        pltpu.make_async_copy(source, target, sems.at[at])
        for at, (source, target) in enumerate(((k_hbm, k_ref), (v_hbm, v_ref)))
    ]
    for copy in copies:
        copy.start()
    groups, tokens, size = k_out.shape
    sign = signs(size)
    for copy, ref, out in zip(copies, (k_ref, v_ref), (k_out, v_out)):
        copy.wait()
        if ref is k_ref:
            rows = nn(k_ref[...], sign) * (1.0 / math.sqrt(size))
        else:
            rows = v_ref[...].astype(F32)
        rows_ref[...] = rows
        for group in range(groups):
            out[group] = rows_ref[pl.ds(group, tokens, stride=groups), :].astype(BF16)


def finish_kernel(count, *refs):
    outs, rows_ref = refs[-3:-1], refs[-1]
    for part, out in enumerate(outs):
        terms = refs[part * count : (part + 1) * count]
        groups, tokens, _ = terms[0].shape
        for group in range(groups):
            rows = [ref[group].astype(F32) for ref in terms]
            rows_ref[pl.ds(group, tokens, stride=groups), :] = sum(rows[1:], rows[0])
        out[...] = rows_ref[...].astype(BF16)


def ring_order(count):
    return [0] + [at for at in range(count) if at % 2] + [at for at in range(count - 1, 0, -1) if at % 2 == 0]


def ring_place(count, place):
    odd = place & 1
    half = place >> 1
    return lax.rem(odd * (half + 1) + (1 - odd) * (count - half), count)


def ring_device(count, ring):
    return jnp.where(ring <= count // 2, jnp.maximum(2 * ring - 1, 0), 2 * (count - ring))


def passed(value, axis, step):
    count = lax.axis_size(axis)
    order = ring_order(count)
    return lax.ppermute(
        value, axis, [(order[at], order[(at + step) % count]) for at in range(count)]
    )


def gather_rest(block, up, down, axis):
    count = lax.axis_size(axis)
    blocks = {0: block, 1: up, count - 1: down}
    for step in range(2, count // 2 + 1):
        up = blocks[step] = passed(up, axis, 1)
        if 2 * step < count:
            down = blocks[count - step] = passed(down, axis, -1)
    return [blocks[step] for step in range(count)]


def passed_down(value, axis):
    count = lax.axis_size(axis)
    return lax.ppermute(value, axis, [(at, (at - 1) % count) for at in range(count)])


def added(a, b):
    return (a.astype(F32) + b.astype(F32)).astype(BF16)


def scatter_sums(parts, axis, relay_after):
    count = lax.axis_size(axis)
    terms, relayed = [parts[0]], []
    for step, longest in ((1, count // 2), (-1, (count - 1) // 2)):
        moving = None
        for distance in range(longest, 0, -1):
            part = parts[(-step * distance) % count]
            if moving is not None:
                moving, _ = lax.optimization_barrier((moving, relay_after))
                part = added(moving, part)
                relayed.append(part)
            moving = passed(part, axis, step)
        terms.append(moving)
    return terms, relayed


def sides_kernel(groups, q_hbm, g_hbm, o_hbm, q_side_ref, g_side_ref, in_ref, sems):
    _, _, half_rows, heads, size = in_ref.shape
    per_group = heads // groups
    copies = []
    for half in range(2):
        for part, source in enumerate((q_hbm, g_hbm, o_hbm)):
            piece = source.at[pl.ds(half * half_rows, half_rows)]
            copies.append(
                pltpu.make_async_copy(piece, in_ref.at[half, part], sems.at[half * 3 + part])
            )
            copies[-1].start()
    rows = half_rows * per_group
    sign = signs(size)
    root = 1.0 / math.sqrt(size)
    row_offset = lax.broadcasted_iota(jnp.int32, (rows, size), 0) // per_group
    lane = lax.broadcasted_iota(jnp.int32, (rows, size), 1)
    hide = jnp.where(row_offset == lane, NEG, 0.0).astype(BF16)
    for half in range(2):
        for copy in copies[3 * half : 3 * half + 3]:
            copy.wait()
        q_all = nn(in_ref[half, 0].reshape(half_rows * heads, size), sign) * root
        q_all = q_all.reshape(half_rows, groups, per_group, size)
        g_all = in_ref[half, 1].astype(F32).reshape(half_rows, groups, per_group, size)
        o_all = in_ref[half, 2].astype(F32).reshape(half_rows, groups, per_group, size)
        for group in range(groups):
            grad = g_all[:, group].reshape(rows, size)
            product = grad * o_all[:, group].reshape(rows, size)
            product = -(product + pltpu.roll(product, size // 2, 1))
            high = product.astype(BF16).astype(F32)
            delta = jnp.where(lane < size // 2, high, product - high)
            q_side_ref[half, group, :, :size] = q_all[:, group].reshape(rows, size).astype(BF16)
            q_side_ref[half, group, :, size:] = hide
            g_side_ref[half, group, :, :size] = grad.astype(BF16)
            g_side_ref[half, group, :, size:] = delta.astype(BF16)


def far_last(count):
    return [step for step in range(count) if step != count // 2] + [count // 2]


def weights_kernel(first, blocks, order_ref, q_side_ref, g_side_ref, *refs):
    k_refs, (weight_ref, scale_ref) = refs[:blocks], refs[blocks : blocks + 2]
    sum_refs, key_ref = refs[blocks + 2 : 2 * blocks + 2], refs[-1]
    groups, keys, _ = weight_ref.shape
    tokens, size = k_refs[0].shape[1:]
    place = lax.axis_index("ctx")
    ring = ring_place(blocks, place)
    rows = q_side_ref.shape[2]
    half_rows = tokens // 2
    power = math.log2(math.e) / math.sqrt(size)

    at_row = lax.broadcasted_iota(jnp.int32, (half_rows, size), 0)
    at_col = lax.broadcasted_iota(jnp.int32, (half_rows, size), 1)
    for block, distance in enumerate(far_last(blocks)):
        source = ring_device(blocks, lax.rem(ring - distance + blocks, blocks))
        for half in range(2):
            q_start = order_ref[place * 2 + half]
            for k_half in range(2):
                ahead = (order_ref[source * 2 + k_half] - q_start) * half_rows
                hidden = (at_row + ahead > at_col) & (at_col < half_rows)
                hidden = jnp.where(hidden, 1.0, 0.0).astype(BF16)
                k_at = pl.ds(block * tokens + k_half * half_rows, half_rows)
                for group in range(groups):
                    key_ref[half, group, k_at, size:] = hidden
        at = pl.ds(block * tokens, tokens)
        for group in range(groups):
            key = k_refs[block][first + group]
            for half in range(2):
                key_ref[half, group, at, :size] = key

    chunk = 256
    units = [(group, half) for group in range(groups) for half in range(2)]
    tops, scales = {}, {}
    for step in range(len(units) + 1):
        top = total = None
        for row in range(0, keys, chunk):
            k_at = pl.ds(row, chunk)
            if step < len(units):
                group, half = units[step]
                part = nt(key_ref[half, group, k_at, :], q_side_ref[half, first + group])
                weight_ref[group, k_at, pl.ds(half * rows, rows)] = part
                part = jnp.max(part.reshape(chunk // 8, 8, rows), axis=0)
                top = part if top is None else jnp.maximum(top, part)
            if step > 0:
                group, half = units[step - 1]
                part = weight_ref[group, k_at, pl.ds(half * rows, rows)]
                part = jnp.exp2((part - tops[step - 1]) * power)
                weight_ref[group, k_at, pl.ds(half * rows, rows)] = part
                part = jnp.sum(part.reshape(chunk // 8, 8, rows), axis=0)
                total = part if total is None else total + part
        if step < len(units):
            tops[step] = jnp.max(top, axis=0, keepdims=True)
        if step > 0:
            group, half = units[step - 1]
            scale = 1.0 / jnp.sum(total, axis=0, keepdims=True)
            scale_ref[group, :, pl.ds(half * rows, rows)] = jnp.broadcast_to(scale, (8, rows))
            scales[half] = scale
        if step == 0 or units[step - 1][1] == 0:
            continue
        for row in range(0, keys, 512):
            dv = None
            for half in range(2):
                probs = weight_ref[group, pl.ds(row, 512), pl.ds(half * rows, rows)] * scales[half]
                part = nn(probs.astype(BF16), g_side_ref[half, first + group, :, :size])
                dv = part if dv is None else dv + part
            dv = dv.astype(BF16)
            for at in range(0, 512, tokens):
                sum_refs[(row + at) // tokens][group] = dv[at : at + tokens]


def dq_kernel(first, blocks, g_side_ref, weight_ref, scale_ref, *refs):
    k_refs, v_refs = refs[:blocks], refs[blocks : 2 * blocks]
    handed_ref, dscore_ref, val_ref, back_ref = refs[2 * blocks :]
    groups, keys, _ = weight_ref.shape
    tokens, size = k_refs[0].shape[1:]
    rows = g_side_ref.shape[2]
    half_rows = tokens // 2
    per_group = rows // half_rows
    chunk = 512
    sign = signs(size)

    for block in range(blocks):
        at = pl.ds(block * tokens, tokens)
        for group in range(groups):
            val_ref[group, at, :size] = v_refs[block][first + group]
            val_ref[group, at, size:] = jnp.ones((tokens, size), BF16)
            high, low = split(nt(sign, k_refs[block][first + group]) * (1.0 / size))
            back_ref[group, :size, at] = high
            back_ref[group, size:, at] = low

    def change(unit, row):
        half, group = unit
        return nt(val_ref[group, pl.ds(row, chunk), :], g_side_ref[half, first + group])

    units = [(half, group) for half in range(2) for group in range(groups)]
    steps = [(unit, row) for unit in units for row in range(0, keys, chunk)]
    ahead = change(*steps[0])
    results, dq = [], None
    for step, ((half, group), row) in enumerate(steps):
        now = ahead
        if step + 1 < len(steps):
            ahead = change(*steps[step + 1])
        k_at, row_at = pl.ds(row, chunk), pl.ds(half * rows, rows)
        probs = weight_ref[group, k_at, row_at] * scale_ref[group, :1, row_at]
        dscore = (probs * now).astype(BF16)
        dscore_ref[group, k_at, row_at] = dscore
        part = nn(back_ref[group, :, k_at], dscore)
        dq = part if dq is None else dq + part
        if row + chunk == keys:
            dq = (dq[:size] + dq[size:]).T + g_side_ref[half, first + group, :, :size].astype(F32)
            results.append(dq.reshape(half_rows, per_group, size))
            dq = None
        if len(results) == groups:
            at = pl.ds(half * half_rows, half_rows)
            handed_ref[at] = jnp.concatenate(results, axis=1).astype(BF16)
            results = []


def dk_kernel(stages, start, q_side_ref, *refs):
    dscore_refs, sum_refs = refs[:stages], refs[stages:]
    tokens, size = sum_refs[0].shape[1:]
    rows = q_side_ref.shape[2]
    signs_twice = jnp.concatenate([signs(size)] * 2, axis=0)
    chunk = 512
    per_stage = dscore_refs[0].shape[0]
    count = len(sum_refs) * tokens
    for row in range(0, count, chunk):
        length = min(chunk, count - row)
        for group in range(stages * per_stage):
            dk = None
            for half in range(2):
                dscore = dscore_refs[group // per_stage].at[group % per_stage]
                dscore = dscore[pl.ds(start * tokens + row, length), pl.ds(half * rows, rows)]
                part = nn(dscore, q_side_ref[half, group, :, :size])
                dk = part if dk is None else dk + part
            dk = (nn(jnp.concatenate(split(dk), axis=1), signs_twice) * (1.0 / size)).astype(BF16)
            for at in range(0, length, tokens):
                sum_refs[(row + at) // tokens][group] = dk[at : at + tokens]


VMEM = pl.BlockSpec(memory_space=pltpu.VMEM)
HBM = pl.BlockSpec(memory_space=pltpu.HBM)
DMA = pltpu.SemaphoreType.DMA
SMEM = pl.BlockSpec(memory_space=pltpu.SMEM)


def call(kernel, name, outs, scratch, limit, work, args, smem=False):
    shapes = [jax.ShapeDtypeStruct(*out) for out in outs]
    return pl.pallas_call(
        kernel,
        in_specs=([SMEM] if smem else []) + [VMEM] * (len(args) - smem),
        out_specs=[VMEM] * len(outs),
        out_shape=shapes,
        scratch_shapes=scratch,
        compiler_params=pltpu.CompilerParams(vmem_limit_bytes=limit * 2**20),
        cost_estimate=pl.CostEstimate(flops=work, bytes_accessed=2**16, transcendentals=0),
        name=name,
    )(*args)


def in_hbm(value):
    return pltpu.with_memory_space_constraint(value, pltpu.HBM)


def make_sides(groups, queries, grads, saved):
    tokens, heads, size = queries.shape
    half_rows = tokens // 2
    rows = half_rows * heads // groups
    shape = jax.ShapeDtypeStruct((2, groups, rows, 2 * size), BF16)
    return pl.pallas_call(
        functools.partial(sides_kernel, groups),
        in_specs=[HBM] * 3,
        out_specs=[VMEM] * 2,
        out_shape=[shape] * 2,
        scratch_shapes=[pltpu.VMEM((2, 3, half_rows, heads, size), BF16), DMA((6,))],
        compiler_params=pltpu.CompilerParams(vmem_limit_bytes=12 * 2**20),
        cost_estimate=pl.CostEstimate(flops=WORK, bytes_accessed=2**16, transcendentals=0),
        name="query_sides",
    )(in_hbm(queries), in_hbm(grads), in_hbm(saved))


def shards(queries, key_heads, value_heads, forward_out, output_grad, block_order):
    _, tokens, groups, size = key_heads.shape
    q_heads = queries.shape[2]
    per_group = q_heads // groups
    per_stage = groups // STAGES
    blocks = lax.axis_size("ctx")
    keys = blocks * tokens
    rows = tokens // 2 * per_group
    packed = ((groups, tokens, size), BF16)
    part = ((per_stage, tokens, size), BF16)
    flat = ((tokens * groups, size), BF16)
    rows_scratch = pltpu.VMEM(*flat[:1], F32)
    limit = 6 + keys // 64
    after = lax.optimization_barrier
    k_block, v_block = pl.pallas_call(
        prep_kernel,
        in_specs=[HBM] * 2,
        out_specs=[VMEM] * 2,
        out_shape=[jax.ShapeDtypeStruct(*packed)] * 2,
        scratch_shapes=[rows_scratch, pltpu.VMEM(*flat), pltpu.VMEM(*flat), DMA((2,))],
        compiler_params=pltpu.CompilerParams(vmem_limit_bytes=8 * 2**20),
        cost_estimate=pl.CostEstimate(flops=WORK, bytes_accessed=2**16, transcendentals=0),
        name="pack_keys",
    )(in_hbm(key_heads.reshape(-1, size)), in_hbm(value_heads.reshape(-1, size)))

    up, down = passed(k_block, "ctx", 1), passed(k_block, "ctx", -1)
    q_loads, _ = after((queries[0], up))
    q_side, g_side = make_sides(groups, q_loads, output_grad[0], forward_out[0])
    k_all = gather_rest(k_block, up, down, "ctx")
    v_block, _ = after((v_block, q_side))
    up, down = passed(v_block, "ctx", 1), passed(v_block, "ctx", -1)

    slots = far_last(blocks)
    k_all = [k_all[step] for step in slots]
    weights, dv_parts = [], []
    for stage in range(STAGES):
        weight, scale, *parts = call(
            functools.partial(weights_kernel, stage * per_stage, blocks),
            "weights",
            [((per_stage, keys, 2 * rows), F32), ((per_stage, 8, 2 * rows), F32)] + [part] * blocks,
            [pltpu.VMEM((2, per_stage, keys, 2 * size), BF16)],
            limit,
            BIG_WORK,
            [block_order, q_side, g_side, *k_all],
            True,
        )
        if stage == 0:
            up, q_side = after((up, q_side, scale))[:2]
            v_all = gather_rest(v_block, up, down, "ctx")
        weights.append((weight, scale))
        dv_parts.append(parts)

    v_all = [v_all[step] for step in slots]
    handed, dscores = [], []
    for stage in range(STAGES):
        handed_part, dscore = call(
            functools.partial(dq_kernel, stage * per_stage, blocks),
            "query_grads",
            [((tokens, per_stage * per_group, size), BF16)]
            + [((per_stage, keys, 2 * rows), BF16)],
            [
                pltpu.VMEM((per_stage, keys, 2 * size), BF16),
                pltpu.VMEM((per_stage, 2 * size, keys), BF16),
            ],
            limit,
            BIG_WORK,
            [g_side, *weights[stage], *k_all, *v_all],
        )
        if stage == 0:
            g_side, _ = after((g_side, handed_part))
        handed.append(passed_down(handed_part, "pipe"))
        dscores.append(dscore)
    dv_parts = [jnp.concatenate(parts, axis=0) for parts in zip(*dv_parts)]
    dv_parts = [dv_parts[slots.index(step)] for step in range(blocks)]
    dv_terms, dv_relayed = scatter_sums(dv_parts, "ctx", ())

    dscores, _ = after((dscores, (dv_relayed, dv_terms[-1])))
    dk_parts = call(
        functools.partial(dk_kernel, STAGES, 0),
        "key_grads",
        [packed] * blocks,
        [],
        limit,
        WORK,
        [q_side, *dscores],
    )
    dk_parts = [dk_parts[slots.index(step)] for step in range(blocks)]
    dk_terms, _ = scatter_sums(dk_parts, "ctx", ())
    handed = jnp.concatenate(handed, axis=1)[None]
    last = lax.axis_index("pipe") == lax.axis_size("pipe") - 1
    handed = jnp.where(last, jnp.zeros_like(handed), handed)
    key_grad, value_grad = call(
        functools.partial(finish_kernel, len(dk_terms)),
        "lay_out",
        [flat, flat],
        [rows_scratch],
        8,
        WORK,
        [*dk_terms, *dv_terms],
    )
    shape = key_heads.shape
    return (
        key_grad.reshape(shape),
        value_grad.reshape(shape),
        handed,
    )


def solution(mesh):
    placed = P("pipe", "ctx", "head", None)
    return jax.shard_map(
        shards,
        mesh=mesh,
        in_specs=(placed,) * 5 + (P(),),
        out_specs=(placed,) * 3,
        check_vma=False,
    )
```

```python
import functools
import math

import jax
import jax.numpy as jnp
from jax import lax
from jax.experimental import pallas as pl
from jax.experimental.pallas import tpu as pltpu
from jax.sharding import PartitionSpec as P

NEG = -1e30
STAGES = 2
WORK = 2**20
BIG_WORK = 2**32
F32 = jnp.float32
BF16 = jnp.bfloat16


def signs(size):
    row = lax.broadcasted_iota(jnp.int32, (size, size), 0)
    col = lax.broadcasted_iota(jnp.int32, (size, size), 1)
    bits = row & col
    for step in (4, 2, 1):
        bits = bits ^ (bits >> step)
    return (1 - 2 * (bits & 1)).astype(F32).astype(BF16)


def dot(a, b, contract):
    return lax.dot_general(a, b, (contract, ((), ())), preferred_element_type=F32)


def nn(a, b):
    return dot(a, b, ((1,), (0,)))


def nt(a, b):
    return dot(a, b, ((1,), (1,)))


def split(x):
    high = x.astype(BF16)
    return high, (x - high.astype(F32)).astype(BF16)


def prep_kernel(k_hbm, v_hbm, k_out, v_out, rows_ref, k_ref, v_ref, sems):
    copies = [
        pltpu.make_async_copy(source, target, sems.at[at])
        for at, (source, target) in enumerate(((k_hbm, k_ref), (v_hbm, v_ref)))
    ]
    for copy in copies:
        copy.start()
    groups, tokens, size = k_out.shape
    sign = signs(size)
    for copy, ref, out in zip(copies, (k_ref, v_ref), (k_out, v_out)):
        copy.wait()
        if ref is k_ref:
            rows = nn(k_ref[...], sign) * (1.0 / math.sqrt(size))
        else:
            rows = v_ref[...].astype(F32)
        rows_ref[...] = rows
        for group in range(groups):
            out[group] = rows_ref[pl.ds(group, tokens, stride=groups), :].astype(BF16)


def finish_kernel(count, *refs):
    outs, rows_ref = refs[-3:-1], refs[-1]
    for part, out in enumerate(outs):
        terms = refs[part * count : (part + 1) * count]
        groups, tokens, _ = terms[0].shape
        for group in range(groups):
            rows = [ref[group].astype(F32) for ref in terms]
            rows_ref[pl.ds(group, tokens, stride=groups), :] = sum(rows[1:], rows[0])
        out[...] = rows_ref[...].astype(BF16)


def ring_order(count):
    return [0] + [at for at in range(count) if at % 2] + [at for at in range(count - 1, 0, -1) if at % 2 == 0]


def ring_place(count, place):
    odd = place & 1
    half = place >> 1
    return lax.rem(odd * (half + 1) + (1 - odd) * (count - half), count)


def ring_device(count, ring):
    return jnp.where(ring <= count // 2, jnp.maximum(2 * ring - 1, 0), 2 * (count - ring))


def passed(value, axis, step):
    count = lax.axis_size(axis)
    order = ring_order(count)
    return lax.ppermute(
        value, axis, [(order[at], order[(at + step) % count]) for at in range(count)]
    )


def gather_rest(block, up, down, axis):
    count = lax.axis_size(axis)
    blocks = {0: block, 1: up, count - 1: down}
    for step in range(2, count // 2 + 1):
        up = blocks[step] = passed(up, axis, 1)
        if 2 * step < count:
            down = blocks[count - step] = passed(down, axis, -1)
    return [blocks[step] for step in range(count)]


def passed_down(value, axis):
    count = lax.axis_size(axis)
    return lax.ppermute(value, axis, [(at, (at - 1) % count) for at in range(count)])


def added(a, b):
    return (a.astype(F32) + b.astype(F32)).astype(BF16)


def scatter_sums(parts, axis, relay_after):
    count = lax.axis_size(axis)
    terms, relayed = [parts[0]], []
    for step, longest in ((1, count // 2), (-1, (count - 1) // 2)):
        moving = None
        for distance in range(longest, 0, -1):
            part = parts[(-step * distance) % count]
            if moving is not None:
                moving, _ = lax.optimization_barrier((moving, relay_after))
                part = added(moving, part)
                relayed.append(part)
            moving = passed(part, axis, step)
        terms.append(moving)
    return terms, relayed


def sides_kernel(groups, q_hbm, g_hbm, o_hbm, q_side_ref, g_side_ref, in_ref, sems):
    _, _, half_rows, heads, size = in_ref.shape
    per_group = heads // groups
    copies = []
    for half in range(2):
        for part, source in enumerate((q_hbm, g_hbm, o_hbm)):
            piece = source.at[pl.ds(half * half_rows, half_rows)]
            copies.append(
                pltpu.make_async_copy(piece, in_ref.at[half, part], sems.at[half * 3 + part])
            )
            copies[-1].start()
    rows = half_rows * per_group
    sign = signs(size)
    root = 1.0 / math.sqrt(size)
    row_offset = lax.broadcasted_iota(jnp.int32, (rows, size), 0) // per_group
    lane = lax.broadcasted_iota(jnp.int32, (rows, size), 1)
    hide = jnp.where(row_offset == lane, NEG, 0.0).astype(BF16)
    for half in range(2):
        for copy in copies[3 * half : 3 * half + 3]:
            copy.wait()
        q_all = nn(in_ref[half, 0].reshape(half_rows * heads, size), sign) * root
        q_all = q_all.reshape(half_rows, groups, per_group, size)
        g_all = in_ref[half, 1].astype(F32).reshape(half_rows, groups, per_group, size)
        o_all = in_ref[half, 2].astype(F32).reshape(half_rows, groups, per_group, size)
        for group in range(groups):
            grad = g_all[:, group].reshape(rows, size)
            product = grad * o_all[:, group].reshape(rows, size)
            product = -(product + pltpu.roll(product, size // 2, 1))
            high = product.astype(BF16).astype(F32)
            delta = jnp.where(lane < size // 2, high, product - high)
            q_side_ref[half, group, :, :size] = q_all[:, group].reshape(rows, size).astype(BF16)
            q_side_ref[half, group, :, size:] = hide
            g_side_ref[half, group, :, :size] = grad.astype(BF16)
            g_side_ref[half, group, :, size:] = delta.astype(BF16)


def far_last(count):
    return [step for step in range(count) if step != count // 2] + [count // 2]


def weights_kernel(first, blocks, order_ref, q_side_ref, g_side_ref, *refs):
    k_refs, (weight_ref, scale_ref) = refs[:blocks], refs[blocks : blocks + 2]
    sum_refs, mask_ref = refs[blocks + 2 : 2 * blocks + 2], refs[-1]
    groups, keys, _ = weight_ref.shape
    tokens, size = k_refs[0].shape[1:]
    place = lax.axis_index("ctx")
    ring = ring_place(blocks, place)
    rows = q_side_ref.shape[2]
    half_rows = tokens // 2
    power = math.log2(math.e) / math.sqrt(size)

    at_row = lax.broadcasted_iota(jnp.int32, (half_rows, size), 0)
    at_col = lax.broadcasted_iota(jnp.int32, (half_rows, size), 1)
    for block, distance in enumerate(far_last(blocks)):
        source = ring_device(blocks, lax.rem(ring - distance + blocks, blocks))
        for half in range(2):
            q_start = order_ref[place * 2 + half]
            for k_half in range(2):
                ahead = (order_ref[source * 2 + k_half] - q_start) * half_rows
                hidden = (at_row + ahead > at_col) & (at_col < half_rows)
                hidden = jnp.where(hidden, 1.0, 0.0).astype(BF16)
                k_at = pl.ds(block * tokens + k_half * half_rows, half_rows)
                mask_ref[half, k_at, :] = hidden

    def key_side(group, half, row):
        near = range(row // tokens, (row + chunk) // tokens)
        keys_here = jnp.concatenate([k_refs[block][first + group] for block in near], axis=0)
        return jnp.concatenate([keys_here, mask_ref[half, pl.ds(row, chunk), :]], axis=1)

    chunk = 256
    units = [(group, half) for group in range(groups) for half in range(2)]
    tops, scales = {}, {}
    for step in range(len(units) + 1):
        top = total = None
        for row in range(0, keys, chunk):
            k_at = pl.ds(row, chunk)
            if step < len(units):
                group, half = units[step]
                part = nt(key_side(group, half, row), q_side_ref[half, first + group])
                weight_ref[group, k_at, pl.ds(half * rows, rows)] = part
                part = jnp.max(part.reshape(chunk // 8, 8, rows), axis=0)
                top = part if top is None else jnp.maximum(top, part)
            if step > 0:
                group, half = units[step - 1]
                part = weight_ref[group, k_at, pl.ds(half * rows, rows)]
                part = jnp.exp2((part - tops[step - 1]) * power)
                weight_ref[group, k_at, pl.ds(half * rows, rows)] = part
                part = jnp.sum(part.reshape(chunk // 8, 8, rows), axis=0)
                total = part if total is None else total + part
        if step < len(units):
            tops[step] = jnp.max(top, axis=0, keepdims=True)
        if step > 0:
            group, half = units[step - 1]
            scale = 1.0 / jnp.sum(total, axis=0, keepdims=True)
            scale_ref[group, :, pl.ds(half * rows, rows)] = jnp.broadcast_to(scale, (8, rows))
            scales[half] = scale
        if step == 0 or units[step - 1][1] == 0:
            continue
        for row in range(0, keys, 512):
            dv = None
            for half in range(2):
                probs = weight_ref[group, pl.ds(row, 512), pl.ds(half * rows, rows)] * scales[half]
                part = nn(probs.astype(BF16), g_side_ref[half, first + group, :, :size])
                dv = part if dv is None else dv + part
            dv = dv.astype(BF16)
            for at in range(0, 512, tokens):
                sum_refs[(row + at) // tokens][group] = dv[at : at + tokens]


def dq_kernel(first, blocks, g_side_ref, weight_ref, scale_ref, *refs):
    k_refs, v_refs = refs[:blocks], refs[blocks : 2 * blocks]
    handed_ref, dscore_ref, back_ref = refs[2 * blocks :]
    groups, keys, _ = weight_ref.shape
    tokens, size = k_refs[0].shape[1:]
    rows = g_side_ref.shape[2]
    half_rows = tokens // 2
    per_group = rows // half_rows
    chunk = 512
    sign = signs(size)

    for block in range(blocks):
        at = pl.ds(block * tokens, tokens)
        for group in range(groups):
            high, low = split(nt(sign, k_refs[block][first + group]) * (1.0 / size))
            back_ref[group, :size, at] = high
            back_ref[group, size:, at] = low

    def change(unit, row):
        half, group = unit
        near = range(row // tokens, (row + chunk) // tokens)
        values = jnp.concatenate([v_refs[block][first + group] for block in near], axis=0)
        values = jnp.concatenate([values, jnp.ones_like(values)], axis=1)
        return nt(values, g_side_ref[half, first + group])

    units = [(half, group) for half in range(2) for group in range(groups)]
    steps = [(unit, row) for unit in units for row in range(0, keys, chunk)]
    ahead = change(*steps[0])
    results, dq = [], None
    for step, ((half, group), row) in enumerate(steps):
        now = ahead
        if step + 1 < len(steps):
            ahead = change(*steps[step + 1])
        k_at, row_at = pl.ds(row, chunk), pl.ds(half * rows, rows)
        probs = weight_ref[group, k_at, row_at] * scale_ref[group, :1, row_at]
        dscore = (probs * now).astype(BF16)
        dscore_ref[group, k_at, row_at] = dscore
        part = nn(back_ref[group, :, k_at], dscore)
        dq = part if dq is None else dq + part
        if row + chunk == keys:
            dq = (dq[:size] + dq[size:]).T + g_side_ref[half, first + group, :, :size].astype(F32)
            results.append(dq.reshape(half_rows, per_group, size))
            dq = None
        if len(results) == groups:
            at = pl.ds(half * half_rows, half_rows)
            handed_ref[at] = jnp.concatenate(results, axis=1).astype(BF16)
            results = []


def dk_kernel(stages, start, q_side_ref, *refs):
    dscore_refs, sum_refs = refs[:stages], refs[stages:]
    tokens, size = sum_refs[0].shape[1:]
    rows = q_side_ref.shape[2]
    signs_twice = jnp.concatenate([signs(size)] * 2, axis=0)
    chunk = 512
    per_stage = dscore_refs[0].shape[0]
    count = len(sum_refs) * tokens
    for row in range(0, count, chunk):
        length = min(chunk, count - row)
        for group in range(stages * per_stage):
            dk = None
            for half in range(2):
                dscore = dscore_refs[group // per_stage].at[group % per_stage]
                dscore = dscore[pl.ds(start * tokens + row, length), pl.ds(half * rows, rows)]
                part = nn(dscore, q_side_ref[half, group, :, :size])
                dk = part if dk is None else dk + part
            dk = (nn(jnp.concatenate(split(dk), axis=1), signs_twice) * (1.0 / size)).astype(BF16)
            for at in range(0, length, tokens):
                sum_refs[(row + at) // tokens][group] = dk[at : at + tokens]


VMEM = pl.BlockSpec(memory_space=pltpu.VMEM)
HBM = pl.BlockSpec(memory_space=pltpu.HBM)
DMA = pltpu.SemaphoreType.DMA
SMEM = pl.BlockSpec(memory_space=pltpu.SMEM)


def call(kernel, name, outs, scratch, limit, work, args, smem=False):
    shapes = [jax.ShapeDtypeStruct(*out) for out in outs]
    return pl.pallas_call(
        kernel,
        in_specs=([SMEM] if smem else []) + [VMEM] * (len(args) - smem),
        out_specs=[VMEM] * len(outs),
        out_shape=shapes,
        scratch_shapes=scratch,
        compiler_params=pltpu.CompilerParams(vmem_limit_bytes=limit * 2**20),
        cost_estimate=pl.CostEstimate(flops=work, bytes_accessed=2**16, transcendentals=0),
        name=name,
    )(*args)


def in_hbm(value):
    return pltpu.with_memory_space_constraint(value, pltpu.HBM)


def make_sides(groups, queries, grads, saved):
    tokens, heads, size = queries.shape
    half_rows = tokens // 2
    rows = half_rows * heads // groups
    shape = jax.ShapeDtypeStruct((2, groups, rows, 2 * size), BF16)
    return pl.pallas_call(
        functools.partial(sides_kernel, groups),
        in_specs=[HBM] * 3,
        out_specs=[VMEM] * 2,
        out_shape=[shape] * 2,
        scratch_shapes=[pltpu.VMEM((2, 3, half_rows, heads, size), BF16), DMA((6,))],
        compiler_params=pltpu.CompilerParams(vmem_limit_bytes=12 * 2**20),
        cost_estimate=pl.CostEstimate(flops=WORK, bytes_accessed=2**16, transcendentals=0),
        name="query_sides",
    )(in_hbm(queries), in_hbm(grads), in_hbm(saved))


def shards(queries, key_heads, value_heads, forward_out, output_grad, block_order):
    _, tokens, groups, size = key_heads.shape
    q_heads = queries.shape[2]
    per_group = q_heads // groups
    per_stage = groups // STAGES
    blocks = lax.axis_size("ctx")
    keys = blocks * tokens
    rows = tokens // 2 * per_group
    packed = ((groups, tokens, size), BF16)
    part = ((per_stage, tokens, size), BF16)
    flat = ((tokens * groups, size), BF16)
    rows_scratch = pltpu.VMEM(*flat[:1], F32)
    limit = 6 + keys // 64
    after = lax.optimization_barrier
    k_block, v_block = pl.pallas_call(
        prep_kernel,
        in_specs=[HBM] * 2,
        out_specs=[VMEM] * 2,
        out_shape=[jax.ShapeDtypeStruct(*packed)] * 2,
        scratch_shapes=[rows_scratch, pltpu.VMEM(*flat), pltpu.VMEM(*flat), DMA((2,))],
        compiler_params=pltpu.CompilerParams(vmem_limit_bytes=8 * 2**20),
        cost_estimate=pl.CostEstimate(flops=WORK, bytes_accessed=2**16, transcendentals=0),
        name="pack_keys",
    )(in_hbm(key_heads.reshape(-1, size)), in_hbm(value_heads.reshape(-1, size)))

    up, down = passed(k_block, "ctx", 1), passed(k_block, "ctx", -1)
    q_loads, _ = after((queries[0], up))
    q_side, g_side = make_sides(groups, q_loads, output_grad[0], forward_out[0])
    k_all = gather_rest(k_block, up, down, "ctx")
    v_block, _ = after((v_block, q_side))
    up, down = passed(v_block, "ctx", 1), passed(v_block, "ctx", -1)

    slots = far_last(blocks)
    k_all = [k_all[step] for step in slots]
    weights, dv_parts = [], []
    for stage in range(STAGES):
        weight, scale, *parts = call(
            functools.partial(weights_kernel, stage * per_stage, blocks),
            "weights",
            [((per_stage, keys, 2 * rows), F32), ((per_stage, 8, 2 * rows), F32)] + [part] * blocks,
            [pltpu.VMEM((2, keys, size), BF16)],
            limit,
            BIG_WORK,
            [block_order, q_side, g_side, *k_all],
            True,
        )
        if stage == 0:
            up, q_side = after((up, q_side, scale))[:2]
            v_all = gather_rest(v_block, up, down, "ctx")
        weights.append((weight, scale))
        dv_parts.append(parts)

    v_all = [v_all[step] for step in slots]
    handed, dscores = [], []
    for stage in range(STAGES):
        handed_part, dscore = call(
            functools.partial(dq_kernel, stage * per_stage, blocks),
            "query_grads",
            [((tokens, per_stage * per_group, size), BF16)]
            + [((per_stage, keys, 2 * rows), BF16)],
            [
                pltpu.VMEM((per_stage, 2 * size, keys), BF16),
            ],
            limit,
            BIG_WORK,
            [g_side, *weights[stage], *k_all, *v_all],
        )
        if stage == 0:
            g_side, _ = after((g_side, handed_part))
            first_handed = handed_part
        handed.append(passed_down(handed_part, "pipe"))
        dscores.append(dscore)
    dv_parts = [jnp.concatenate(parts, axis=0) for parts in zip(*dv_parts)]
    dv_parts = [dv_parts[slots.index(step)] for step in range(blocks)]
    dv_parts[1], _ = after((dv_parts[1], first_handed))
    dv_terms, dv_relayed = scatter_sums(dv_parts, "ctx", ())

    dscores, _ = after((dscores, (dv_relayed, dv_terms[-1])))
    dk_parts = call(
        functools.partial(dk_kernel, STAGES, 0),
        "key_grads",
        [packed] * blocks,
        [],
        limit,
        WORK,
        [q_side, *dscores],
    )
    dk_parts = [dk_parts[slots.index(step)] for step in range(blocks)]
    dk_terms, _ = scatter_sums(dk_parts, "ctx", ())
    handed = jnp.concatenate(handed, axis=1)[None]
    last = lax.axis_index("pipe") == lax.axis_size("pipe") - 1
    handed = jnp.where(last, jnp.zeros_like(handed), handed)
    key_grad, value_grad = call(
        functools.partial(finish_kernel, len(dk_terms)),
        "lay_out",
        [flat, flat],
        [rows_scratch],
        8,
        WORK,
        [*dk_terms, *dv_terms],
    )
    shape = key_heads.shape
    return (
        key_grad.reshape(shape),
        value_grad.reshape(shape),
        handed,
    )


def solution(mesh):
    placed = P("pipe", "ctx", "head", None)
    return jax.shard_map(
        shards,
        mesh=mesh,
        in_specs=(placed,) * 5 + (P(),),
        out_specs=(placed,) * 3,
        check_vma=False,
    )
```

```python
import functools
import math

import jax
import jax.numpy as jnp
from jax import lax
from jax.experimental import pallas as pl
from jax.experimental.pallas import tpu as pltpu
from jax.sharding import PartitionSpec as P

NEG = -1e30
STAGES = 2
WORK = 2**20
BIG_WORK = 2**32
F32 = jnp.float32
BF16 = jnp.bfloat16


def signs(size):
    row = lax.broadcasted_iota(jnp.int32, (size, size), 0)
    col = lax.broadcasted_iota(jnp.int32, (size, size), 1)
    bits = row & col
    for step in (4, 2, 1):
        bits = bits ^ (bits >> step)
    return (1 - 2 * (bits & 1)).astype(F32).astype(BF16)


def dot(a, b, contract):
    return lax.dot_general(a, b, (contract, ((), ())), preferred_element_type=F32)


def nn(a, b):
    return dot(a, b, ((1,), (0,)))


def nt(a, b):
    return dot(a, b, ((1,), (1,)))


def split(x):
    high = x.astype(BF16)
    return high, (x - high.astype(F32)).astype(BF16)


def prep_kernel(k_hbm, v_hbm, k_out, v_out, rows_ref, k_ref, v_ref, sems):
    copies = [
        pltpu.make_async_copy(source, target, sems.at[at])
        for at, (source, target) in enumerate(((k_hbm, k_ref), (v_hbm, v_ref)))
    ]
    for copy in copies:
        copy.start()
    groups, tokens, size = k_out.shape
    sign = signs(size)
    for copy, ref, out in zip(copies, (k_ref, v_ref), (k_out, v_out)):
        copy.wait()
        if ref is k_ref:
            rows = nn(k_ref[...], sign) * (1.0 / math.sqrt(size))
        else:
            rows = v_ref[...].astype(F32)
        rows_ref[...] = rows
        for group in range(groups):
            out[group] = rows_ref[pl.ds(group, tokens, stride=groups), :].astype(BF16)


def finish_kernel(count, *refs):
    outs, rows_ref = refs[-3:-1], refs[-1]
    for part, out in enumerate(outs):
        terms = refs[part * count : (part + 1) * count]
        groups, tokens, _ = terms[0].shape
        for group in range(groups):
            rows = [ref[group].astype(F32) for ref in terms]
            rows_ref[pl.ds(group, tokens, stride=groups), :] = sum(rows[1:], rows[0])
        out[...] = rows_ref[...].astype(BF16)


def ring_order(count):
    return [0] + [at for at in range(count) if at % 2] + [at for at in range(count - 1, 0, -1) if at % 2 == 0]


def ring_place(count, place):
    odd = place & 1
    half = place >> 1
    return lax.rem(odd * (half + 1) + (1 - odd) * (count - half), count)


def ring_device(count, ring):
    return jnp.where(ring <= count // 2, jnp.maximum(2 * ring - 1, 0), 2 * (count - ring))


def passed(value, axis, step):
    count = lax.axis_size(axis)
    order = ring_order(count)
    return lax.ppermute(
        value, axis, [(order[at], order[(at + step) % count]) for at in range(count)]
    )


def gather_rest(block, up, down, axis):
    count = lax.axis_size(axis)
    blocks = {0: block, 1: up, count - 1: down}
    for step in range(2, count // 2 + 1):
        up = blocks[step] = passed(up, axis, 1)
        if 2 * step < count:
            down = blocks[count - step] = passed(down, axis, -1)
    return [blocks[step] for step in range(count)]


def passed_down(value, axis):
    count = lax.axis_size(axis)
    return lax.ppermute(value, axis, [(at, (at - 1) % count) for at in range(count)])


def added(a, b):
    return (a.astype(F32) + b.astype(F32)).astype(BF16)


def scatter_sums(parts, axis, relay_after):
    count = lax.axis_size(axis)
    terms, relayed = [parts[0]], []
    for step, longest in ((1, count // 2), (-1, (count - 1) // 2)):
        moving = None
        for distance in range(longest, 0, -1):
            part = parts[(-step * distance) % count]
            if moving is not None:
                moving, _ = lax.optimization_barrier((moving, relay_after))
                part = added(moving, part)
                relayed.append(part)
            moving = passed(part, axis, step)
        terms.append(moving)
    return terms, relayed


def fetch(sources, in_ref, sems):
    half_rows = in_ref.shape[2]
    copies = []
    for half in range(2):
        for part, source in enumerate(sources):
            piece = source.at[pl.ds(half * half_rows, half_rows)]
            sem = sems.at[half * len(sources) + part]
            copies.append(pltpu.make_async_copy(piece, in_ref.at[half, part], sem))
            copies[-1].start()

    def wait(half):
        for copy in copies[half * len(sources) : (half + 1) * len(sources)]:
            copy.wait()

    return wait


def query_side_kernel(groups, q_hbm, side_ref, in_ref, sems):
    wait = fetch((q_hbm,), in_ref, sems)
    _, _, half_rows, heads, size = in_ref.shape
    per_group = heads // groups
    rows = half_rows * per_group
    sign = signs(size)
    row_offset = lax.broadcasted_iota(jnp.int32, (rows, size), 0) // per_group
    lane = lax.broadcasted_iota(jnp.int32, (rows, size), 1)
    hide = jnp.where(row_offset == lane, NEG, 0.0).astype(BF16)
    for half in range(2):
        wait(half)
        q_all = nn(in_ref[half, 0].reshape(half_rows * heads, size), sign) * (1.0 / math.sqrt(size))
        q_all = q_all.reshape(half_rows, groups, per_group, size)
        for group in range(groups):
            side_ref[half, group, :, :size] = q_all[:, group].reshape(rows, size).astype(BF16)
            side_ref[half, group, :, size:] = hide


def grad_side_kernel(groups, g_hbm, o_hbm, side_ref, in_ref, sems):
    wait = fetch((g_hbm, o_hbm), in_ref, sems)
    _, _, half_rows, heads, size = in_ref.shape
    per_group = heads // groups
    rows = half_rows * per_group
    lane = lax.broadcasted_iota(jnp.int32, (rows, size), 1)
    for half in range(2):
        wait(half)
        g_all = in_ref[half, 0].astype(F32).reshape(half_rows, groups, per_group, size)
        o_all = in_ref[half, 1].astype(F32).reshape(half_rows, groups, per_group, size)
        for group in range(groups):
            grad = g_all[:, group].reshape(rows, size)
            product = grad * o_all[:, group].reshape(rows, size)
            product = -(product + pltpu.roll(product, size // 2, 1))
            high = product.astype(BF16).astype(F32)
            delta = jnp.where(lane < size // 2, high, product - high)
            side_ref[half, group, :, :size] = grad.astype(BF16)
            side_ref[half, group, :, size:] = delta.astype(BF16)


def far_last(count):
    return [step for step in range(count) if step != count // 2] + [count // 2]


def weights_kernel(first, blocks, order_ref, q_side_ref, g_side_ref, *refs):
    k_refs, (weight_ref, scale_ref) = refs[:blocks], refs[blocks : blocks + 2]
    sum_refs, mask_ref = refs[blocks + 2 : 2 * blocks + 2], refs[-1]
    groups, keys, _ = weight_ref.shape
    tokens, size = k_refs[0].shape[1:]
    place = lax.axis_index("ctx")
    ring = ring_place(blocks, place)
    rows = q_side_ref.shape[2]
    half_rows = tokens // 2
    power = math.log2(math.e) / math.sqrt(size)

    at_row = lax.broadcasted_iota(jnp.int32, (half_rows, size), 0)
    at_col = lax.broadcasted_iota(jnp.int32, (half_rows, size), 1)
    for block, distance in enumerate(far_last(blocks)):
        source = ring_device(blocks, lax.rem(ring - distance + blocks, blocks))
        for half in range(2):
            q_start = order_ref[place * 2 + half]
            for k_half in range(2):
                ahead = (order_ref[source * 2 + k_half] - q_start) * half_rows
                hidden = (at_row + ahead > at_col) & (at_col < half_rows)
                hidden = jnp.where(hidden, 1.0, 0.0).astype(BF16)
                k_at = pl.ds(block * tokens + k_half * half_rows, half_rows)
                mask_ref[half, k_at, :] = hidden

    def key_side(group, half, row):
        near = range(row // tokens, (row + chunk) // tokens)
        keys_here = jnp.concatenate([k_refs[block][first + group] for block in near], axis=0)
        return jnp.concatenate([keys_here, mask_ref[half, pl.ds(row, chunk), :]], axis=1)

    chunk = 256
    units = [(group, half) for group in range(groups) for half in range(2)]
    tops, scales = {}, {}
    for step in range(len(units) + 1):
        top = total = None
        for row in range(0, keys, chunk):
            k_at = pl.ds(row, chunk)
            if step < len(units):
                group, half = units[step]
                part = nt(key_side(group, half, row), q_side_ref[half, first + group])
                weight_ref[group, k_at, pl.ds(half * rows, rows)] = part
                part = jnp.max(part.reshape(chunk // 8, 8, rows), axis=0)
                top = part if top is None else jnp.maximum(top, part)
            if step > 0:
                group, half = units[step - 1]
                part = weight_ref[group, k_at, pl.ds(half * rows, rows)]
                part = jnp.exp2((part - tops[step - 1]) * power)
                weight_ref[group, k_at, pl.ds(half * rows, rows)] = part
                part = jnp.sum(part.reshape(chunk // 8, 8, rows), axis=0)
                total = part if total is None else total + part
        if step < len(units):
            tops[step] = jnp.max(top, axis=0, keepdims=True)
        if step > 0:
            group, half = units[step - 1]
            scale = 1.0 / jnp.sum(total, axis=0, keepdims=True)
            scale_ref[group, :, pl.ds(half * rows, rows)] = jnp.broadcast_to(scale, (8, rows))
            scales[half] = scale
        if step == 0 or units[step - 1][1] == 0:
            continue
        for row in range(0, keys, 512):
            dv = None
            for half in range(2):
                probs = weight_ref[group, pl.ds(row, 512), pl.ds(half * rows, rows)] * scales[half]
                part = nn(probs.astype(BF16), g_side_ref[half, first + group, :, :size])
                dv = part if dv is None else dv + part
            dv = dv.astype(BF16)
            for at in range(0, 512, tokens):
                sum_refs[(row + at) // tokens][group] = dv[at : at + tokens]


def dq_kernel(first, blocks, g_side_ref, weight_ref, scale_ref, *refs):
    k_refs, v_refs = refs[:blocks], refs[blocks : 2 * blocks]
    handed_ref, dscore_ref, back_ref = refs[2 * blocks :]
    groups, keys, _ = weight_ref.shape
    tokens, size = k_refs[0].shape[1:]
    rows = g_side_ref.shape[2]
    half_rows = tokens // 2
    per_group = rows // half_rows
    chunk = 512
    sign = signs(size)

    for block in range(blocks):
        at = pl.ds(block * tokens, tokens)
        for group in range(groups):
            high, low = split(nt(sign, k_refs[block][first + group]) * (1.0 / size))
            back_ref[group, :size, at] = high
            back_ref[group, size:, at] = low

    def change(unit, row):
        half, group = unit
        near = range(row // tokens, (row + chunk) // tokens)
        values = jnp.concatenate([v_refs[block][first + group] for block in near], axis=0)
        values = jnp.concatenate([values, jnp.ones_like(values)], axis=1)
        return nt(values, g_side_ref[half, first + group])

    units = [(half, group) for half in range(2) for group in range(groups)]
    steps = [(unit, row) for unit in units for row in range(0, keys, chunk)]
    ahead = change(*steps[0])
    results, dq = [], None
    for step, ((half, group), row) in enumerate(steps):
        now = ahead
        if step + 1 < len(steps):
            ahead = change(*steps[step + 1])
        k_at, row_at = pl.ds(row, chunk), pl.ds(half * rows, rows)
        probs = weight_ref[group, k_at, row_at] * scale_ref[group, :1, row_at]
        dscore = (probs * now).astype(BF16)
        dscore_ref[group, k_at, row_at] = dscore
        part = nn(back_ref[group, :, k_at], dscore)
        dq = part if dq is None else dq + part
        if row + chunk == keys:
            dq = (dq[:size] + dq[size:]).T + g_side_ref[half, first + group, :, :size].astype(F32)
            results.append(dq.reshape(half_rows, per_group, size))
            dq = None
        if len(results) == groups:
            at = pl.ds(half * half_rows, half_rows)
            handed_ref[at] = jnp.concatenate(results, axis=1).astype(BF16)
            results = []


def dk_kernel(stages, start, q_side_ref, *refs):
    dscore_refs, sum_refs = refs[:stages], refs[stages:]
    tokens, size = sum_refs[0].shape[1:]
    rows = q_side_ref.shape[2]
    signs_twice = jnp.concatenate([signs(size)] * 2, axis=0)
    chunk = 512
    per_stage = dscore_refs[0].shape[0]
    count = len(sum_refs) * tokens
    for row in range(0, count, chunk):
        length = min(chunk, count - row)
        for group in range(stages * per_stage):
            dk = None
            for half in range(2):
                dscore = dscore_refs[group // per_stage].at[group % per_stage]
                dscore = dscore[pl.ds(start * tokens + row, length), pl.ds(half * rows, rows)]
                part = nn(dscore, q_side_ref[half, group, :, :size])
                dk = part if dk is None else dk + part
            dk = (nn(jnp.concatenate(split(dk), axis=1), signs_twice) * (1.0 / size)).astype(BF16)
            for at in range(0, length, tokens):
                sum_refs[(row + at) // tokens][group] = dk[at : at + tokens]


VMEM = pl.BlockSpec(memory_space=pltpu.VMEM)
HBM = pl.BlockSpec(memory_space=pltpu.HBM)
DMA = pltpu.SemaphoreType.DMA
SMEM = pl.BlockSpec(memory_space=pltpu.SMEM)


def call(kernel, name, outs, scratch, limit, work, args, smem=False):
    shapes = [jax.ShapeDtypeStruct(*out) for out in outs]
    return pl.pallas_call(
        kernel,
        in_specs=([SMEM] if smem else []) + [VMEM] * (len(args) - smem),
        out_specs=[VMEM] * len(outs),
        out_shape=shapes,
        scratch_shapes=scratch,
        compiler_params=pltpu.CompilerParams(vmem_limit_bytes=limit * 2**20),
        cost_estimate=pl.CostEstimate(flops=work, bytes_accessed=2**16, transcendentals=0),
        name=name,
    )(*args)


def in_hbm(value):
    return pltpu.with_memory_space_constraint(value, pltpu.HBM)


def make_side(kernel, name, groups, *sources):
    tokens, heads, size = sources[0].shape
    half_rows = tokens // 2
    rows = half_rows * heads // groups
    count = len(sources)
    return pl.pallas_call(
        functools.partial(kernel, groups),
        in_specs=[HBM] * count,
        out_specs=VMEM,
        out_shape=jax.ShapeDtypeStruct((2, groups, rows, 2 * size), BF16),
        scratch_shapes=[pltpu.VMEM((2, count, half_rows, heads, size), BF16), DMA((2 * count,))],
        compiler_params=pltpu.CompilerParams(vmem_limit_bytes=12 * 2**20),
        cost_estimate=pl.CostEstimate(flops=WORK, bytes_accessed=2**16, transcendentals=0),
        name=name,
    )(*[in_hbm(source) for source in sources])


def shards(queries, key_heads, value_heads, forward_out, output_grad, block_order):
    _, tokens, groups, size = key_heads.shape
    q_heads = queries.shape[2]
    per_group = q_heads // groups
    per_stage = groups // STAGES
    blocks = lax.axis_size("ctx")
    keys = blocks * tokens
    rows = tokens // 2 * per_group
    packed = ((groups, tokens, size), BF16)
    part = ((per_stage, tokens, size), BF16)
    flat = ((tokens * groups, size), BF16)
    rows_scratch = pltpu.VMEM(*flat[:1], F32)
    limit = 6 + keys // 64
    after = lax.optimization_barrier
    k_block, v_block = pl.pallas_call(
        prep_kernel,
        in_specs=[HBM] * 2,
        out_specs=[VMEM] * 2,
        out_shape=[jax.ShapeDtypeStruct(*packed)] * 2,
        scratch_shapes=[rows_scratch, pltpu.VMEM(*flat), pltpu.VMEM(*flat), DMA((2,))],
        compiler_params=pltpu.CompilerParams(vmem_limit_bytes=8 * 2**20),
        cost_estimate=pl.CostEstimate(flops=WORK, bytes_accessed=2**16, transcendentals=0),
        name="pack_keys",
    )(in_hbm(key_heads.reshape(-1, size)), in_hbm(value_heads.reshape(-1, size)))

    up, down = passed(k_block, "ctx", 1), passed(k_block, "ctx", -1)
    g_side = make_side(grad_side_kernel, "grad_side", groups, output_grad[0], forward_out[0])
    up, g_side = after((up, g_side))
    q_loads, _ = after((queries[0], up))
    q_side = make_side(query_side_kernel, "query_side", groups, q_loads)
    k_all = gather_rest(k_block, up, down, "ctx")
    v_block, _ = after((v_block, q_side))
    up, down = passed(v_block, "ctx", 1), passed(v_block, "ctx", -1)

    slots = far_last(blocks)
    k_all = [k_all[step] for step in slots]
    weights, dv_parts = [], []
    for stage in range(STAGES):
        weight, scale, *parts = call(
            functools.partial(weights_kernel, stage * per_stage, blocks),
            "weights",
            [((per_stage, keys, 2 * rows), F32), ((per_stage, 8, 2 * rows), F32)] + [part] * blocks,
            [pltpu.VMEM((2, keys, size), BF16)],
            limit,
            BIG_WORK,
            [block_order, q_side, g_side, *k_all],
            True,
        )
        if stage == 0:
            up, q_side = after((up, q_side, scale))[:2]
            v_all = gather_rest(v_block, up, down, "ctx")
        weights.append((weight, scale))
        dv_parts.append(parts)

    v_all = [v_all[step] for step in slots]
    handed, dscores = [], []
    for stage in range(STAGES):
        handed_part, dscore = call(
            functools.partial(dq_kernel, stage * per_stage, blocks),
            "query_grads",
            [((tokens, per_stage * per_group, size), BF16)]
            + [((per_stage, keys, 2 * rows), BF16)],
            [
                pltpu.VMEM((per_stage, 2 * size, keys), BF16),
            ],
            limit,
            BIG_WORK,
            [g_side, *weights[stage], *k_all, *v_all],
        )
        if stage == 0:
            g_side, _ = after((g_side, handed_part))
        handed.append(passed_down(handed_part, "pipe"))
        dscores.append(dscore)
    dv_parts = [jnp.concatenate(parts, axis=0) for parts in zip(*dv_parts)]
    dv_parts = [dv_parts[slots.index(step)] for step in range(blocks)]
    dv_terms, dv_relayed = scatter_sums(dv_parts, "ctx", ())

    dscores, _ = after((dscores, (dv_relayed, dv_terms[-1])))
    dk_parts = call(
        functools.partial(dk_kernel, STAGES, 0),
        "key_grads",
        [packed] * blocks,
        [],
        limit,
        WORK,
        [q_side, *dscores],
    )
    dk_parts = [dk_parts[slots.index(step)] for step in range(blocks)]
    dk_terms, _ = scatter_sums(dk_parts, "ctx", ())
    handed = jnp.concatenate(handed, axis=1)[None]
    last = lax.axis_index("pipe") == lax.axis_size("pipe") - 1
    handed = jnp.where(last, jnp.zeros_like(handed), handed)
    key_grad, value_grad = call(
        functools.partial(finish_kernel, len(dk_terms)),
        "lay_out",
        [flat, flat],
        [rows_scratch],
        8,
        WORK,
        [*dk_terms, *dv_terms],
    )
    shape = key_heads.shape
    return (
        key_grad.reshape(shape),
        value_grad.reshape(shape),
        handed,
    )


def solution(mesh):
    placed = P("pipe", "ctx", "head", None)
    return jax.shard_map(
        shards,
        mesh=mesh,
        in_specs=(placed,) * 5 + (P(),),
        out_specs=(placed,) * 3,
        check_vma=False,
    )
```

```python
import functools
import math

import jax
import jax.numpy as jnp
from jax import lax
from jax.experimental import pallas as pl
from jax.experimental.pallas import tpu as pltpu
from jax.sharding import PartitionSpec as P

NEG = -1e30
STAGES = 2
WORK = 2**20
BIG_WORK = 2**32
F32 = jnp.float32
BF16 = jnp.bfloat16


def signs(size):
    row = lax.broadcasted_iota(jnp.int32, (size, size), 0)
    col = lax.broadcasted_iota(jnp.int32, (size, size), 1)
    bits = row & col
    for step in (4, 2, 1):
        bits = bits ^ (bits >> step)
    return (1 - 2 * (bits & 1)).astype(F32).astype(BF16)


def dot(a, b, contract):
    return lax.dot_general(a, b, (contract, ((), ())), preferred_element_type=F32)


def nn(a, b):
    return dot(a, b, ((1,), (0,)))


def nt(a, b):
    return dot(a, b, ((1,), (1,)))


def split(x):
    high = x.astype(BF16)
    return high, (x - high.astype(F32)).astype(BF16)


def prep_kernel(k_hbm, v_hbm, k_out, v_out, rows_ref, k_ref, v_ref, sems):
    copies = [
        pltpu.make_async_copy(source, target, sems.at[at])
        for at, (source, target) in enumerate(((k_hbm, k_ref), (v_hbm, v_ref)))
    ]
    for copy in copies:
        copy.start()
    groups, tokens, size = k_out.shape
    sign = signs(size)
    for copy, ref, out in zip(copies, (k_ref, v_ref), (k_out, v_out)):
        copy.wait()
        if ref is k_ref:
            rows = nn(k_ref[...], sign) * (1.0 / math.sqrt(size))
        else:
            rows = v_ref[...].astype(F32)
        rows_ref[...] = rows
        for group in range(groups):
            out[group] = rows_ref[pl.ds(group, tokens, stride=groups), :].astype(BF16)


def finish_kernel(count, *refs):
    outs, rows_ref = refs[-3:-1], refs[-1]
    for part, out in enumerate(outs):
        terms = refs[part * count : (part + 1) * count]
        groups, tokens, _ = terms[0].shape
        for group in range(groups):
            rows = [ref[group].astype(F32) for ref in terms]
            rows_ref[pl.ds(group, tokens, stride=groups), :] = sum(rows[1:], rows[0])
        out[...] = rows_ref[...].astype(BF16)


def ring_order(count):
    return [0] + [at for at in range(count) if at % 2] + [at for at in range(count - 1, 0, -1) if at % 2 == 0]


def ring_place(count, place):
    odd = place & 1
    half = place >> 1
    return lax.rem(odd * (half + 1) + (1 - odd) * (count - half), count)


def ring_device(count, ring):
    return jnp.where(ring <= count // 2, jnp.maximum(2 * ring - 1, 0), 2 * (count - ring))


def passed(value, axis, step):
    count = lax.axis_size(axis)
    order = ring_order(count)
    return lax.ppermute(
        value, axis, [(order[at], order[(at - step) % count]) for at in range(count)]
    )


def gather_rest(block, up, down, axis):
    count = lax.axis_size(axis)
    blocks = {0: block, 1: up, count - 1: down}
    for step in range(2, count // 2 + 1):
        up = blocks[step] = passed(up, axis, 1)
        if 2 * step < count:
            down = blocks[count - step] = passed(down, axis, -1)
    return [blocks[step] for step in range(count)]


def passed_down(value, axis):
    count = lax.axis_size(axis)
    return lax.ppermute(value, axis, [(at, (at - 1) % count) for at in range(count)])


def added(a, b):
    return (a.astype(F32) + b.astype(F32)).astype(BF16)


def scatter_sums(parts, axis, relay_after):
    count = lax.axis_size(axis)
    terms, relayed = [parts[0]], []
    for step, longest in ((1, count // 2), (-1, (count - 1) // 2)):
        moving = None
        for distance in range(longest, 0, -1):
            part = parts[(-step * distance) % count]
            if moving is not None:
                moving, _ = lax.optimization_barrier((moving, relay_after))
                part = added(moving, part)
                relayed.append(part)
            moving = passed(part, axis, step)
        terms.append(moving)
    return terms, relayed


def fetch(sources, in_ref, sems):
    half_rows = in_ref.shape[2]
    copies = []
    for half in range(2):
        for part, source in enumerate(sources):
            piece = source.at[pl.ds(half * half_rows, half_rows)]
            sem = sems.at[half * len(sources) + part]
            copies.append(pltpu.make_async_copy(piece, in_ref.at[half, part], sem))
            copies[-1].start()

    def wait(half):
        for copy in copies[half * len(sources) : (half + 1) * len(sources)]:
            copy.wait()

    return wait


def query_side_kernel(groups, q_hbm, side_ref, in_ref, sems):
    wait = fetch((q_hbm,), in_ref, sems)
    _, _, half_rows, heads, size = in_ref.shape
    per_group = heads // groups
    rows = half_rows * per_group
    sign = signs(size)
    row_offset = lax.broadcasted_iota(jnp.int32, (rows, size), 0) // per_group
    lane = lax.broadcasted_iota(jnp.int32, (rows, size), 1)
    hide = jnp.where(row_offset == lane, NEG, 0.0).astype(BF16)
    for half in range(2):
        wait(half)
        q_all = nn(in_ref[half, 0].reshape(half_rows * heads, size), sign) * (1.0 / math.sqrt(size))
        q_all = q_all.reshape(half_rows, groups, per_group, size)
        for group in range(groups):
            side_ref[half, group, :, :size] = q_all[:, group].reshape(rows, size).astype(BF16)
            side_ref[half, group, :, size:] = hide


def grad_side_kernel(groups, g_hbm, o_hbm, side_ref, in_ref, sems):
    wait = fetch((g_hbm, o_hbm), in_ref, sems)
    _, _, half_rows, heads, size = in_ref.shape
    per_group = heads // groups
    rows = half_rows * per_group
    lane = lax.broadcasted_iota(jnp.int32, (rows, size), 1)
    for half in range(2):
        wait(half)
        g_all = in_ref[half, 0].astype(F32).reshape(half_rows, groups, per_group, size)
        o_all = in_ref[half, 1].astype(F32).reshape(half_rows, groups, per_group, size)
        for group in range(groups):
            grad = g_all[:, group].reshape(rows, size)
            product = grad * o_all[:, group].reshape(rows, size)
            product = -(product + pltpu.roll(product, size // 2, 1))
            high = product.astype(BF16).astype(F32)
            delta = jnp.where(lane < size // 2, high, product - high)
            side_ref[half, group, :, :size] = grad.astype(BF16)
            side_ref[half, group, :, size:] = delta.astype(BF16)


def far_last(count):
    return [step for step in range(count) if step != count // 2] + [count // 2]


def weights_kernel(first, blocks, order_ref, q_side_ref, g_side_ref, *refs):
    k_refs, (weight_ref, scale_ref) = refs[:blocks], refs[blocks : blocks + 2]
    sum_refs, mask_ref = refs[blocks + 2 : 2 * blocks + 2], refs[-1]
    groups, keys, _ = weight_ref.shape
    tokens, size = k_refs[0].shape[1:]
    place = lax.axis_index("ctx")
    ring = ring_place(blocks, place)
    rows = q_side_ref.shape[2]
    half_rows = tokens // 2
    power = math.log2(math.e) / math.sqrt(size)

    at_row = lax.broadcasted_iota(jnp.int32, (half_rows, size), 0)
    at_col = lax.broadcasted_iota(jnp.int32, (half_rows, size), 1)
    for block, distance in enumerate(far_last(blocks)):
        source = ring_device(blocks, lax.rem(ring + distance, blocks))
        for half in range(2):
            q_start = order_ref[place * 2 + half]
            for k_half in range(2):
                ahead = (order_ref[source * 2 + k_half] - q_start) * half_rows
                hidden = (at_row + ahead > at_col) & (at_col < half_rows)
                hidden = jnp.where(hidden, 1.0, 0.0).astype(BF16)
                k_at = pl.ds(block * tokens + k_half * half_rows, half_rows)
                mask_ref[half, k_at, :] = hidden

    def key_side(group, half, row):
        near = range(row // tokens, (row + chunk) // tokens)
        keys_here = jnp.concatenate([k_refs[block][first + group] for block in near], axis=0)
        return jnp.concatenate([keys_here, mask_ref[half, pl.ds(row, chunk), :]], axis=1)

    chunk = 256
    units = [(group, half) for group in range(groups) for half in range(2)]
    tops, scales = {}, {}
    for step in range(len(units) + 1):
        top = total = None
        for row in range(0, keys, chunk):
            k_at = pl.ds(row, chunk)
            if step < len(units):
                group, half = units[step]
                part = nt(key_side(group, half, row), q_side_ref[half, first + group])
                weight_ref[group, k_at, pl.ds(half * rows, rows)] = part
                part = jnp.max(part.reshape(chunk // 8, 8, rows), axis=0)
                top = part if top is None else jnp.maximum(top, part)
            if step > 0:
                group, half = units[step - 1]
                part = weight_ref[group, k_at, pl.ds(half * rows, rows)]
                part = jnp.exp2((part - tops[step - 1]) * power)
                weight_ref[group, k_at, pl.ds(half * rows, rows)] = part
                part = jnp.sum(part.reshape(chunk // 8, 8, rows), axis=0)
                total = part if total is None else total + part
        if step < len(units):
            tops[step] = jnp.max(top, axis=0, keepdims=True)
        if step > 0:
            group, half = units[step - 1]
            scale = 1.0 / jnp.sum(total, axis=0, keepdims=True)
            scale_ref[group, :, pl.ds(half * rows, rows)] = jnp.broadcast_to(scale, (8, rows))
            scales[half] = scale
        if step == 0 or units[step - 1][1] == 0:
            continue
        for row in range(0, keys, 512):
            dv = None
            for half in range(2):
                probs = weight_ref[group, pl.ds(row, 512), pl.ds(half * rows, rows)] * scales[half]
                part = nn(probs.astype(BF16), g_side_ref[half, first + group, :, :size])
                dv = part if dv is None else dv + part
            dv = dv.astype(BF16)
            for at in range(0, 512, tokens):
                sum_refs[(row + at) // tokens][group] = dv[at : at + tokens]


def dq_kernel(first, blocks, g_side_ref, weight_ref, scale_ref, *refs):
    k_refs, v_refs = refs[:blocks], refs[blocks : 2 * blocks]
    handed_ref, dscore_ref, back_ref = refs[2 * blocks :]
    groups, keys, _ = weight_ref.shape
    tokens, size = k_refs[0].shape[1:]
    rows = g_side_ref.shape[2]
    half_rows = tokens // 2
    per_group = rows // half_rows
    chunk = 512
    sign = signs(size)

    for block in range(blocks):
        at = pl.ds(block * tokens, tokens)
        for group in range(groups):
            high, low = split(nt(sign, k_refs[block][first + group]) * (1.0 / size))
            back_ref[group, :size, at] = high
            back_ref[group, size:, at] = low

    def change(unit, row):
        half, group = unit
        near = range(row // tokens, (row + chunk) // tokens)
        values = jnp.concatenate([v_refs[block][first + group] for block in near], axis=0)
        values = jnp.concatenate([values, jnp.ones_like(values)], axis=1)
        return nt(values, g_side_ref[half, first + group])

    units = [(half, group) for half in range(2) for group in range(groups)]
    steps = [(unit, row) for unit in units for row in range(0, keys, chunk)]
    ahead = change(*steps[0])
    results, dq = [], None
    for step, ((half, group), row) in enumerate(steps):
        now = ahead
        if step + 1 < len(steps):
            ahead = change(*steps[step + 1])
        k_at, row_at = pl.ds(row, chunk), pl.ds(half * rows, rows)
        probs = weight_ref[group, k_at, row_at] * scale_ref[group, :1, row_at]
        dscore = (probs * now).astype(BF16)
        dscore_ref[group, k_at, row_at] = dscore
        part = nn(back_ref[group, :, k_at], dscore)
        dq = part if dq is None else dq + part
        if row + chunk == keys:
            dq = (dq[:size] + dq[size:]).T + g_side_ref[half, first + group, :, :size].astype(F32)
            results.append(dq.reshape(half_rows, per_group, size))
            dq = None
        if len(results) == groups:
            at = pl.ds(half * half_rows, half_rows)
            handed_ref[at] = jnp.concatenate(results, axis=1).astype(BF16)
            results = []


def dk_kernel(stages, start, q_side_ref, *refs):
    dscore_refs, sum_refs = refs[:stages], refs[stages:]
    tokens, size = sum_refs[0].shape[1:]
    rows = q_side_ref.shape[2]
    signs_twice = jnp.concatenate([signs(size)] * 2, axis=0)
    chunk = 512
    per_stage = dscore_refs[0].shape[0]
    count = len(sum_refs) * tokens
    for row in range(0, count, chunk):
        length = min(chunk, count - row)
        for group in range(stages * per_stage):
            dk = None
            for half in range(2):
                dscore = dscore_refs[group // per_stage].at[group % per_stage]
                dscore = dscore[pl.ds(start * tokens + row, length), pl.ds(half * rows, rows)]
                part = nn(dscore, q_side_ref[half, group, :, :size])
                dk = part if dk is None else dk + part
            dk = (nn(jnp.concatenate(split(dk), axis=1), signs_twice) * (1.0 / size)).astype(BF16)
            for at in range(0, length, tokens):
                sum_refs[(row + at) // tokens][group] = dk[at : at + tokens]


VMEM = pl.BlockSpec(memory_space=pltpu.VMEM)
HBM = pl.BlockSpec(memory_space=pltpu.HBM)
DMA = pltpu.SemaphoreType.DMA
SMEM = pl.BlockSpec(memory_space=pltpu.SMEM)


def call(kernel, name, outs, scratch, limit, work, args, smem=False):
    shapes = [jax.ShapeDtypeStruct(*out) for out in outs]
    return pl.pallas_call(
        kernel,
        in_specs=([SMEM] if smem else []) + [VMEM] * (len(args) - smem),
        out_specs=[VMEM] * len(outs),
        out_shape=shapes,
        scratch_shapes=scratch,
        compiler_params=pltpu.CompilerParams(vmem_limit_bytes=limit * 2**20),
        cost_estimate=pl.CostEstimate(flops=work, bytes_accessed=2**16, transcendentals=0),
        name=name,
    )(*args)


def in_hbm(value):
    return pltpu.with_memory_space_constraint(value, pltpu.HBM)


def make_side(kernel, name, groups, *sources):
    tokens, heads, size = sources[0].shape
    half_rows = tokens // 2
    rows = half_rows * heads // groups
    count = len(sources)
    return pl.pallas_call(
        functools.partial(kernel, groups),
        in_specs=[HBM] * count,
        out_specs=VMEM,
        out_shape=jax.ShapeDtypeStruct((2, groups, rows, 2 * size), BF16),
        scratch_shapes=[pltpu.VMEM((2, count, half_rows, heads, size), BF16), DMA((2 * count,))],
        compiler_params=pltpu.CompilerParams(vmem_limit_bytes=12 * 2**20),
        cost_estimate=pl.CostEstimate(flops=WORK, bytes_accessed=2**16, transcendentals=0),
        name=name,
    )(*[in_hbm(source) for source in sources])


def shards(queries, key_heads, value_heads, forward_out, output_grad, block_order):
    _, tokens, groups, size = key_heads.shape
    q_heads = queries.shape[2]
    per_group = q_heads // groups
    per_stage = groups // STAGES
    blocks = lax.axis_size("ctx")
    keys = blocks * tokens
    rows = tokens // 2 * per_group
    packed = ((groups, tokens, size), BF16)
    part = ((per_stage, tokens, size), BF16)
    flat = ((tokens * groups, size), BF16)
    rows_scratch = pltpu.VMEM(*flat[:1], F32)
    limit = 6 + keys // 64
    after = lax.optimization_barrier
    k_block, v_block = pl.pallas_call(
        prep_kernel,
        in_specs=[HBM] * 2,
        out_specs=[VMEM] * 2,
        out_shape=[jax.ShapeDtypeStruct(*packed)] * 2,
        scratch_shapes=[rows_scratch, pltpu.VMEM(*flat), pltpu.VMEM(*flat), DMA((2,))],
        compiler_params=pltpu.CompilerParams(vmem_limit_bytes=8 * 2**20),
        cost_estimate=pl.CostEstimate(flops=WORK, bytes_accessed=2**16, transcendentals=0),
        name="pack_keys",
    )(in_hbm(key_heads.reshape(-1, size)), in_hbm(value_heads.reshape(-1, size)))

    up, down = passed(k_block, "ctx", 1), passed(k_block, "ctx", -1)
    g_side = make_side(grad_side_kernel, "grad_side", groups, output_grad[0], forward_out[0])
    up, g_side = after((up, g_side))
    q_loads, _ = after((queries[0], up))
    q_side = make_side(query_side_kernel, "query_side", groups, q_loads)
    k_all = gather_rest(k_block, up, down, "ctx")
    v_block, _ = after((v_block, q_side))
    up, down = passed(v_block, "ctx", 1), passed(v_block, "ctx", -1)

    slots = far_last(blocks)
    k_all = [k_all[step] for step in slots]
    weights, dv_parts = [], []
    for stage in range(STAGES):
        weight, scale, *parts = call(
            functools.partial(weights_kernel, stage * per_stage, blocks),
            "weights",
            [((per_stage, keys, 2 * rows), F32), ((per_stage, 8, 2 * rows), F32)] + [part] * blocks,
            [pltpu.VMEM((2, keys, size), BF16)],
            limit,
            BIG_WORK,
            [block_order, q_side, g_side, *k_all],
            True,
        )
        if stage == 0:
            up, q_side = after((up, q_side, scale))[:2]
            v_all = gather_rest(v_block, up, down, "ctx")
        weights.append((weight, scale))
        dv_parts.append(parts)

    v_all = [v_all[step] for step in slots]
    handed, dscores = [], []
    for stage in range(STAGES):
        handed_part, dscore = call(
            functools.partial(dq_kernel, stage * per_stage, blocks),
            "query_grads",
            [((tokens, per_stage * per_group, size), BF16)]
            + [((per_stage, keys, 2 * rows), BF16)],
            [
                pltpu.VMEM((per_stage, 2 * size, keys), BF16),
            ],
            limit,
            BIG_WORK,
            [g_side, *weights[stage], *k_all, *v_all],
        )
        if stage == 0:
            g_side, _ = after((g_side, handed_part))
        handed.append(passed_down(handed_part, "pipe"))
        dscores.append(dscore)
    dv_parts = [jnp.concatenate(parts, axis=0) for parts in zip(*dv_parts)]
    dv_parts = [dv_parts[slots.index(step)] for step in range(blocks)]
    dv_terms, dv_relayed = scatter_sums(dv_parts, "ctx", ())

    dscores, _ = after((dscores, (dv_relayed, dv_terms[-1])))
    dk_parts = call(
        functools.partial(dk_kernel, STAGES, 0),
        "key_grads",
        [packed] * blocks,
        [],
        limit,
        WORK,
        [q_side, *dscores],
    )
    dk_parts = [dk_parts[slots.index(step)] for step in range(blocks)]
    dk_terms, _ = scatter_sums(dk_parts, "ctx", ())
    handed = jnp.concatenate(handed, axis=1)[None]
    last = lax.axis_index("pipe") == lax.axis_size("pipe") - 1
    handed = jnp.where(last, jnp.zeros_like(handed), handed)
    key_grad, value_grad = call(
        functools.partial(finish_kernel, len(dk_terms)),
        "lay_out",
        [flat, flat],
        [rows_scratch],
        8,
        WORK,
        [*dk_terms, *dv_terms],
    )
    shape = key_heads.shape
    return (
        key_grad.reshape(shape),
        value_grad.reshape(shape),
        handed,
    )


def solution(mesh):
    placed = P("pipe", "ctx", "head", None)
    return jax.shard_map(
        shards,
        mesh=mesh,
        in_specs=(placed,) * 5 + (P(),),
        out_specs=(placed,) * 3,
        check_vma=False,
    )
```
